32 devices in a mesh: dp: 16 (over z, y, core), mp: 2 (over x).
Axes of the slice: x: 2, y: 2, z: 4, core: 2. Of those that a mesh axis runs over, the one named last changes fastest.
Arguments:
- context: bfloat16 [2, 4096, 1920], P(None, 'dp'), may hold values from -6 to 6
- cotangent: bfloat16 [2, 4096, 1600], P(None, 'dp', 'mp'), may hold values from -6 to 6
- tile_counts: int32 [16], P('dp'), may hold values from 1 to 4
- momentum: float32 [2, 1920, 1600], P(None, 'dp', 'mp'), may hold values from -6 to 6
- weights: float32 [2, 1920, 1600], P(None, 'dp', 'mp'), may hold values from -0.625 to 0.625
Outputs:
- new_momentum: float32 [2, 1920, 1600], P(None, 'dp', 'mp')
- new_weights: float32 [2, 1920, 1600], P(None, 'dp', 'mp')
The draws below stay inside these ranges and needn't reach their ends.
Inputs may be any that keep to these rules, and one draw needn't show every extreme that they name: `tile_counts`: tiles of an image at or past its count are padding.
All inputs are finite; a program needn't handle non-finite values.
Results may differ from the reference program's by a relative error of at most 0.0018.
Values may be sent and summed in bfloat16 or wider, within the bound.
No kernel may reach another device: no remote copies, remote signals or barrier semaphores. Data moves between devices by JAX's collectives and lax.ppermute only.
A program may use at most 128 MiB of HBM per device.

```python
import math
import jax
import jax.numpy as jnp
from jax import lax

HEAD = 128
HEADS_WIN = 15
COLS = 1600
LAYERS = 2
ITERS = 3
TILES = 4
TILE_TOK = 64
ROWS = 1920
TOK_DEV = 256
IMAGES = 16
TOKENS = 4096


def plant(drawn, key, least, largest):
    index_at = [jax.random.randint(jax.random.fold_in(key, axis), (), 0, length) for axis, length in enumerate(drawn.shape)]
    main_axis = drawn.shape.index(max(drawn.shape))
    neighbour = index_at[:main_axis] + [(index_at[main_axis] + 1) % drawn.shape[main_axis]] + index_at[main_axis + 1:]
    return drawn.at[tuple(index_at)].set(least).at[tuple(neighbour)].set(largest)


def with_spikes(result, key, source, target, parts, factor):
    def block_of(dim):
        return (jnp.arange(result.shape[dim]) // (result.shape[dim] // parts)).reshape((-1,) + (1,) * (result.ndim - 1 - dim))

    first = jax.random.permutation(key, parts)[block_of(target)]
    other_side = (block_of(target) + parts // 2) % parts
    return jnp.where((block_of(source) == first) | (block_of(source) == other_side), factor * result, result)


def steps_of(stream_key, dims, split, low, largest):
    gain, own = 1.0, jax.random.fold_in(stream_key, 6)
    for dim, shards_of in split:
        steps = jnp.exp(jax.random.uniform(jax.random.fold_in(own, dim), (shards_of,), jnp.float32, low / len(split), largest / len(split)))
        gain = gain * jnp.repeat(steps, dims[dim] // shards_of).reshape([-1 if axis == dim else 1 for axis in range(len(dims))])
    return gain


def normal_values(own_key, shape, spread, bound, pieces=(), kind=jnp.bfloat16):
    loudness = steps_of(own_key, shape, pieces, -0.22, 0.18) if pieces else 1.0
    drawn = jax.random.normal(own_key, shape, jnp.float32) * spread * loudness
    return jnp.minimum(jnp.maximum(drawn, -bound), bound).astype(kind)


def bell_draw_with(stream_key, extent, deviation, bound, cuts, heavy, kind=jnp.bfloat16):
    drawn = deviation * jax.random.normal(stream_key, extent, jnp.float32)
    if cuts:
        drawn = drawn * steps_of(stream_key, extent, cuts, -0.22, 0.18)
    return jnp.clip(with_spikes(drawn, jax.random.fold_in(stream_key, 3), *heavy), -bound, bound).astype(kind)


def setup_inputs(seed: int = 0) -> dict:
    key_of = jax.random.split(jax.random.key(seed), 6)
    return {
        "context": bell_draw_with(key_of[0], (LAYERS, TOKENS, ROWS), 1.0, 6.0, ((1, 16),), (1, 2, 16, 2.0)),
        "cotangent": normal_values(key_of[1], (LAYERS, TOKENS, COLS), 1.0, 6.0, ((1, 16), (2, 2))),
        "tile_counts": plant(jax.random.randint(key_of[2], (IMAGES,), 1, TILES + 1), jax.random.fold_in(key_of[2], 1), 1, TILES).astype(jnp.int32),
        "momentum": normal_values(key_of[3], (LAYERS, ROWS, COLS), 1.0, 6.0, ((1, 16), (2, 2)), jnp.float32),
        "weights": normal_values(key_of[4], (LAYERS, ROWS, COLS), 0.04, 0.625, ((1, 16), (2, 2)), jnp.float32),
    }


quintic_a = 3.4445
quintic_b = -4.775
quintic_c = 2.0315
momentum_rate = 0.95
learn_rate = 0.02
weight_decay = 0.1
norm_floor = 1e-07

def orthogonalize(slab_block):
    widened = slab_block.astype(jnp.float32)
    sum_squares = lax.optimization_barrier(jnp.sum(widened * widened, axis=(1, 2), keepdims=True))
    current = (widened / (jnp.sqrt(sum_squares) + norm_floor)).astype(jnp.bfloat16)
    for step_index in range(ITERS):
        values = current.astype(jnp.float32)
        gram_matrix = jnp.einsum('hrc,hsc->hrs', values, values).astype(jnp.bfloat16)
        gram_wide = gram_matrix.astype(jnp.float32)
        square = jnp.einsum('hrs,hst->hrt', gram_wide, gram_wide)
        poly_term = (quintic_b * gram_wide + quintic_c * square).astype(jnp.bfloat16)
        current = (quintic_a * values + jnp.einsum('hrs,hsc->hrc', poly_term.astype(jnp.float32), values)).astype(jnp.bfloat16)
    return current

def reference(context, cotangent, tile_counts, momentum, weights):
    position = jnp.arange(TOKENS, dtype=jnp.int32)
    image_index = position // TOK_DEV
    tile_slot = position % TOK_DEV // TILE_TOK
    live_mask = (tile_slot < tile_counts[image_index]).astype(cotangent.dtype)
    masked = cotangent * live_mask[None, :, None]
    factor = 1.0 / math.sqrt(TOKENS)
    update_scale = 0.2 * math.sqrt(max(HEAD, COLS))
    moments = []
    updated = []
    for layer_index in range(LAYERS):
        gradient = lax.dot_general(context[layer_index], masked[layer_index], (((0,), (0,)), ((), ())), preferred_element_type=jnp.float32) * factor
        moment_new = momentum_rate * momentum[layer_index] + gradient
        nesterov = (gradient + momentum_rate * moment_new).astype(jnp.bfloat16)
        blocks = jnp.transpose(nesterov.reshape(HEAD, HEADS_WIN, COLS), (1, 0, 2))
        ortho_blocks = orthogonalize(blocks)
        ortho = jnp.transpose(ortho_blocks, (1, 0, 2)).reshape(ROWS, COLS)
        layer_weights = weights[layer_index]
        new_layer = layer_weights - learn_rate * (weight_decay * layer_weights + update_scale * ortho.astype(jnp.float32))
        moments.append(moment_new)
        updated.append(new_layer)
    return (jnp.stack(moments), jnp.stack(updated))
```

```python
import functools
import math

import jax
import jax.numpy as jnp
from jax import lax
from jax.experimental import pallas as pl
from jax.experimental.pallas import tpu as pltpu
from jax.sharding import PartitionSpec as P

HEAD = 128
HEADS_WIN = 15
COLS = 1600
ITERS = 3
TILE_TOK = 64


quintic_a = 3.4445
quintic_b = -4.775
quintic_c = 2.0315
momentum_rate = 0.95
learn_rate = 0.02
weight_decay = 0.1
norm_floor = 1e-07

SIZE_Z, SIZE_Y, SIZE_C = 4, 2, 2
GAIN = 1.0 + momentum_rate
MIX = momentum_rate * momentum_rate / GAIN
BF16 = jnp.bfloat16
F32 = jnp.float32
VMEM_BYTES = 48 * 1024 * 1024


def quintic(current, reduce_gram):
    for step_index in range(ITERS):
        partial_value = jnp.einsum(
            "lshc,lsgc->lshg", current, current, preferred_element_type=jnp.float32
        )
        gram_matrix = reduce_gram(partial_value).astype(jnp.bfloat16)
        square = jnp.einsum(
            "lshg,lsgk->lshk", gram_matrix, gram_matrix, preferred_element_type=jnp.float32
        )
        poly_term = (quintic_b * gram_matrix.astype(jnp.float32) + quintic_c * square).astype(
            jnp.bfloat16
        )
        product = jnp.einsum(
            "lshg,lsgc->lshc", poly_term, current, preferred_element_type=jnp.float32
        )
        current = (quintic_a * current.astype(jnp.float32) + product).astype(jnp.bfloat16)
    return current


def row_plan(context, cotangent, tile_counts, momentum, weights):
    layers, tok_dev, all_rows = context.shape
    columns = cotangent.shape[2]
    shard_rows = momentum.shape[1]
    position = lax.broadcasted_iota(jnp.int32, (tok_dev, 1), 0)
    live_mask = (position // TILE_TOK < tile_counts[0]).astype(cotangent.dtype)
    masked = cotangent * live_mask[None]
    factor = 1.0 / math.sqrt(tok_dev * lax.axis_size("dp"))

    def layer_term(layer_index):
        block = context[layer_index]
        return (
            lax.dot_general(
                block,
                masked[layer_index],
                (((0,), (0,)), ((), ())),
                preferred_element_type=jnp.float32,
            )
            * factor
        )

    pieces = []
    for layer_index in range(layers):

        def one_term(first_row, row_count, chosen=layer_index):
            return layer_term(chosen)

        pieces.append(
            lax.psum_scatter(
                one_term(jnp.int32(0), lax.axis_size("dp") * shard_rows),
                "dp",
                scatter_dimension=0,
                tiled=True,
            )
        )
    gradient = jnp.stack(pieces)
    moment_new = momentum_rate * momentum + gradient
    nesterov = (gradient + momentum_rate * moment_new).astype(jnp.bfloat16)
    row_start = lax.axis_index("dp") * shard_rows
    slots = min(shard_rows, HEADS_WIN)
    head_ids = (row_start + lax.broadcasted_iota(jnp.int32, (slots,), 0)) % HEADS_WIN
    gathered = lax.all_gather(nesterov, "dp", axis=1, tiled=True)
    grid = gathered.reshape(layers, HEAD, HEADS_WIN, columns)
    slab_block = jnp.transpose(jnp.take(grid, head_ids, axis=2), (0, 2, 1, 3))
    widened = slab_block.astype(jnp.float32)
    sum_squares = lax.psum(jnp.sum(widened * widened, axis=(2, 3)), "mp")
    current = (widened / (jnp.sqrt(sum_squares) + norm_floor)[:, :, None, None]).astype(
        jnp.bfloat16
    )
    orthogonal = quintic(
        current,
        lambda partial_value: lax.psum(partial_value.astype(jnp.bfloat16), "mp").astype(
            jnp.float32
        ),
    )
    local_rows = lax.broadcasted_iota(jnp.int32, (shard_rows,), 0)
    global_rows = row_start + local_rows
    flat_index = local_rows % HEADS_WIN * HEAD + global_rows // HEADS_WIN
    update_rows = jnp.take(
        orthogonal.reshape(layers, slots * HEAD, columns), flat_index, axis=1
    ).astype(jnp.float32)
    update_scale = 0.2 * math.sqrt(max(HEAD, COLS))
    new_weights = weights - learn_rate * (weight_decay * weights + update_scale * update_rows)
    return (moment_new, new_weights)

def dp_index(z, y, c):
    return (z * SIZE_Y + y) * SIZE_C + c


def all_chips():
    return [(z, y, c) for z in range(SIZE_Z) for y in range(SIZE_Y) for c in range(SIZE_C)]


def swap_core(value):
    return lax.ppermute(value, "dp", [(dp_index(z, y, c), dp_index(z, y, 1 - c)) for z, y, c in all_chips()])


def swap_y(value):
    return lax.ppermute(value, "dp", [(dp_index(z, y, c), dp_index(z, 1 - y, c)) for z, y, c in all_chips()])


def swap_x(value):
    return lax.ppermute(value, "mp", [(0, 1), (1, 0)])


def after(value, *earlier):
    return lax.optimization_barrier((value, *earlier))[0]


def contract(left, right, dims):
    return lax.dot_general(left, right, (dims, ((), ())), preferred_element_type=F32)


def own_kernel(ctx0, ctx1, ext0, ext1, perm, hot, out_ref):
    total = None
    for source, (ctx, ext) in enumerate(((ctx0, ext0), (ctx1, ext1))):
        ordered = contract(ctx[...], perm[...], ((1,), (0,))).astype(BF16)
        tokens = jnp.concatenate([ordered, hot[source]], axis=0)
        term = contract(ext[...], tokens, ((1,), (0,)))
        total = term if total is None else total + term
    out_ref[0] = total


def other_kernel(side, first0, second0, first1, second1, ext0, ext1, perm, hot, partial, out_ref, *, factor):
    half = first0.shape[0]
    near = pl.multiple_of(side[0] * half, half)
    far = pl.multiple_of((1 - side[0]) * half, half)
    total = partial[0]
    for source, (first, second, ext) in enumerate(((first0, second0, ext0), (first1, second1, ext1))):
        rows_near = contract(first[...], perm[...], ((1,), (0,))).astype(BF16)
        rows_far = contract(second[...], perm[...], ((1,), (0,))).astype(BF16)
        total += contract(ext[:, pl.ds(near, half)], rows_near, ((1,), (0,)))
        total += contract(ext[:, pl.ds(far, half)], rows_far, ((1,), (0,)))
        total += contract(ext[:, 2 * half :], hot[source], ((1,), (0,)))
    out_ref[0] = total * factor


def gram_kernel(mixed, nesterov_ref, gram_ref, turned_ref):
    value = mixed[...]
    nesterov = (GAIN * value).astype(BF16)
    nesterov_ref[...] = nesterov
    for head in range(2):
        block = nesterov[:, head * HEAD : (head + 1) * HEAD]
        gram_ref[head] = contract(block, block, ((0,), (0,)))
    turned_ref[...] = value.T


def square_dot(left, right):
    return jnp.dot(left, right, precision=lax.Precision.HIGHEST, preferred_element_type=F32)


def ortho_kernel(near, far, nesterov, out_ref):
    row = lax.broadcasted_iota(jnp.int32, (HEAD, HEAD), 0)
    column = lax.broadcasted_iota(jnp.int32, (HEAD, HEAD), 1)
    eye = (row == column).astype(F32)
    for head in range(2):
        raw = near[head] + far[head]
        squares = jnp.sum(raw * eye, axis=(0, 1), keepdims=True)
        scale = 1.0 / (jnp.sqrt(squares) + norm_floor)
        gram = raw * (scale * scale)
        total = None
        for step in range(ITERS):
            poly = quintic_b * gram + quintic_c * square_dot(gram, gram)
            factor = quintic_a * eye + poly
            total = factor if total is None else square_dot(factor, total)
            if step + 1 < ITERS:
                gram = square_dot(square_dot(factor, gram), factor)
        total = total * scale
        high = total.astype(BF16)
        low = (total - high.astype(F32)).astype(BF16)
        block = nesterov[:, head * HEAD : (head + 1) * HEAD]
        out_ref[pl.ds(head * HEAD, HEAD), :] = contract(high, block, ((1,), (1,))) + contract(low, block, ((1,), (1,)))


def final_kernel(back, order, momentum, mixed_in, weights, momentum_ref, weights_ref, *, update_scale):
    for layer in range(2):
        pieces = [back[z, layer, c] for z in range(SIZE_Z) for c in range(SIZE_C)]
        summed = jnp.concatenate([piece[0] for piece in pieces], axis=0)
        ortho = jnp.concatenate([piece[1] for piece in pieces], axis=0).astype(BF16)
        high = summed.astype(BF16)
        low = (summed - high.astype(F32)).astype(BF16)
        rows = momentum.shape[2]
        mixed = contract(high, order[...], ((0,), (0,))) + contract(low, order[...], ((0,), (0,)))
        update = contract(ortho, order[...], ((0,), (0,)))
        gradient = mixed[:, :rows] - 0.5 * mixed_in[layer].astype(F32)
        momentum_ref[layer] = momentum_rate * momentum[layer] + gradient
        old = weights[layer]
        weights_ref[layer] = old - learn_rate * (weight_decay * old + update_scale * update[:, :rows])


def vmem_params(**kwargs):
    return pltpu.CompilerParams(vmem_limit_bytes=VMEM_BYTES, **kwargs)


def block_plan(context, cotangent, tile_counts, momentum, weights):
    layers, tok_dev, all_rows = context.shape
    columns = cotangent.shape[2]
    shard_rows = momentum.shape[1]
    depth = shard_rows // HEADS_WIN
    half = tok_dev // 2
    where = lax.axis_index("dp")
    z, y, c = where // (SIZE_Y * SIZE_C), where // SIZE_C % SIZE_Y, where % SIZE_C
    x = lax.axis_index("mp")
    factor = 1.0 / math.sqrt(tok_dev * lax.axis_size("dp"))

    position = lax.broadcasted_iota(jnp.int32, (1, 1, tok_dev), 2)
    live_mask = (position // TILE_TOK < tile_counts[0]).astype(cotangent.dtype)
    masked = jnp.transpose(cotangent, (0, 2, 1)) * live_mask
    momentum_t = jnp.transpose(momentum, (0, 2, 1))
    weights_t = jnp.transpose(weights, (0, 2, 1))
    mixed_in = (momentum_t * (2.0 * MIX)).astype(BF16)
    pad = HEAD - shard_rows
    ext = jnp.concatenate([masked, mixed_in, jnp.zeros((layers, columns, pad), BF16)], axis=2)

    ctx_keep = lax.dynamic_index_in_dim(context, y, 0, False)
    ext_keep = lax.dynamic_index_in_dim(ext, y, 0, False)
    ext_send = lax.dynamic_index_in_dim(ext, 1 - y, 0, False)
    half_send = lax.dynamic_slice(context, (1 - y, x * half, 0), (1, half, all_rows))[0]

    first0 = swap_y(half_send)
    ctx1 = swap_core(ctx_keep)
    ext1 = swap_core(ext_keep)
    ext2 = swap_y(ext_send)
    second0 = swap_x(first0)
    first1 = swap_core(first0)
    second1 = swap_core(second0)
    ext3 = swap_core(ext2)

    slot_cols = SIZE_Z * 2 * HEAD
    row = lax.broadcasted_iota(jnp.int32, (all_rows, slot_cols), 0)
    col = lax.broadcasted_iota(jnp.int32, (all_rows, slot_cols), 1)
    head = col // (2 * HEAD) * 4 + c * 2 + col // HEAD % 2
    perm = ((row == col % HEAD * HEADS_WIN + head) & (head < HEADS_WIN)).astype(BF16)
    shape = (4, HEAD, slot_cols)
    sender = lax.broadcasted_iota(jnp.int32, shape, 0)
    sender_y = jnp.where(sender // 2 == 0, y, 1 - y)
    sender_c = jnp.where(sender % 2 == 0, c, 1 - c)
    local = lax.broadcasted_iota(jnp.int32, shape, 1)
    col = lax.broadcasted_iota(jnp.int32, shape, 2)
    head = col // (2 * HEAD) * 4 + c * 2 + col // HEAD % 2
    from_row = dp_index(z, sender_y, sender_c) * shard_rows + local
    hit = (from_row == col % HEAD * HEADS_WIN + head) & (head < HEADS_WIN) & (local < shard_rows)
    hot = jnp.where(hit, 0.5 / factor, 0.0).astype(BF16)

    whole = lambda *shape: pl.BlockSpec(shape, lambda j: (0,) * len(shape))
    lanes = 2 * HEAD
    perm_spec = pl.BlockSpec((all_rows, lanes), lambda j: (0, j))
    chunk_spec = pl.BlockSpec((1, columns, lanes), lambda j: (j, 0, 0))
    chunks = jax.ShapeDtypeStruct((SIZE_Z, columns, lanes), F32)
    wide = tok_dev + HEAD
    partial = pl.pallas_call(
        own_kernel,
        grid=(SIZE_Z,),
        in_specs=[whole(tok_dev, all_rows)] * 2
        + [whole(columns, wide)] * 2
        + [perm_spec, pl.BlockSpec((2, HEAD, lanes), lambda j: (0, 0, j))],
        out_specs=chunk_spec,
        out_shape=chunks,
        compiler_params=vmem_params(),
        cost_estimate=pl.CostEstimate(flops=6 * 10**9, bytes_accessed=10**7, transcendentals=0),
    )(ctx_keep, ctx1, ext_keep, ext1, perm, hot)
    total = pl.pallas_call(
        functools.partial(other_kernel, factor=factor),
        grid=(SIZE_Z,),
        in_specs=[pl.BlockSpec(memory_space=pltpu.SMEM)]
        + [whole(half, all_rows)] * 4
        + [whole(columns, wide)] * 2
        + [perm_spec, pl.BlockSpec((2, HEAD, lanes), lambda j: (1, 0, j)), chunk_spec],
        out_specs=chunk_spec,
        out_shape=chunks,
        compiler_params=vmem_params(),
        cost_estimate=pl.CostEstimate(flops=6 * 10**9, bytes_accessed=10**7, transcendentals=0),
    )(x.reshape(1), first0, second0, first1, second1, ext2, ext3, perm, hot, partial)

    groups = [[dp_index(k, b, a) for k in range(SIZE_Z)] for b in range(SIZE_Y) for a in range(SIZE_C)]
    arrived = lax.all_to_all(total.astype(jnp.float16), "dp", 0, 0, axis_index_groups=groups)
    mixed = jnp.sum(arrived.astype(F32), axis=0)

    nesterov, gram, turned = pl.pallas_call(
        gram_kernel,
        out_shape=(
            jax.ShapeDtypeStruct((columns, lanes), BF16),
            jax.ShapeDtypeStruct((2, HEAD, HEAD), F32),
            jax.ShapeDtypeStruct((lanes, columns), F32),
        ),
        compiler_params=vmem_params(),
    )(mixed)
    ortho = pl.pallas_call(
        ortho_kernel,
        out_shape=jax.ShapeDtypeStruct((lanes, columns), F32),
        compiler_params=vmem_params(),
    )(gram, swap_x(gram), nesterov)

    def by_owner(value):
        value = value.astype(jnp.float16).reshape(2, lax.axis_size("dp"), depth, columns)
        return jnp.transpose(value, (1, 0, 2, 3)).reshape(-1, 1, 2 * depth, columns)

    sent = jnp.concatenate([by_owner(turned), by_owner(ortho)], axis=1)
    back = lax.all_to_all(sent, "dp", 0, 0).astype(F32)
    back = back.reshape(SIZE_Z, SIZE_Y, SIZE_C, 2, 2 * depth, columns)

    count = SIZE_Z * SIZE_C * 2 * depth
    row = lax.broadcasted_iota(jnp.int32, (count, HEAD), 0)
    col = lax.broadcasted_iota(jnp.int32, (count, HEAD), 1)
    order = ((col == row % depth * HEADS_WIN + row // depth) & (row // depth < HEADS_WIN)).astype(BF16)
    out = jax.ShapeDtypeStruct((layers, columns, shard_rows), F32)
    moment_new, new_weights = pl.pallas_call(
        functools.partial(final_kernel, update_scale=0.2 * math.sqrt(max(HEAD, COLS))),
        out_shape=(out, out),
        compiler_params=vmem_params(),
    )(back, order, momentum_t, mixed_in, weights_t)
    return jnp.transpose(moment_new, (0, 2, 1)), jnp.transpose(new_weights, (0, 2, 1))


def solution(mesh):
    in_specs = (
        P(None, "dp", None),
        P(None, "dp", "mp"),
        P("dp"),
        P(None, "dp", "mp"),
        P(None, "dp", "mp"),
    )
    out_specs = (P(None, "dp", "mp"), P(None, "dp", "mp"))
    small = mesh.shape["dp"] == SIZE_Z * SIZE_Y * SIZE_C and mesh.shape["mp"] == 2
    return jax.shard_map(
        block_plan if small else row_plan, mesh=mesh, in_specs=in_specs, out_specs=out_specs, check_vma=False
    )
```

```python
import functools
import math

import jax
import jax.numpy as jnp
from jax import lax
from jax.experimental import pallas as pl
from jax.experimental.pallas import tpu as pltpu
from jax.sharding import PartitionSpec as P

HEAD = 128
HEADS_WIN = 15
COLS = 1600
ITERS = 3
TILE_TOK = 64


quintic_a = 3.4445
quintic_b = -4.775
quintic_c = 2.0315
momentum_rate = 0.95
learn_rate = 0.02
weight_decay = 0.1
norm_floor = 1e-07

SIZE_Z, SIZE_Y, SIZE_C = 4, 2, 2
GAIN = 1.0 + momentum_rate
MIX = momentum_rate * momentum_rate / GAIN
BF16 = jnp.bfloat16
F32 = jnp.float32
VMEM_BYTES = 48 * 1024 * 1024


def quintic(current, reduce_gram):
    for step_index in range(ITERS):
        partial_value = jnp.einsum(
            "lshc,lsgc->lshg", current, current, preferred_element_type=jnp.float32
        )
        gram_matrix = reduce_gram(partial_value).astype(jnp.bfloat16)
        square = jnp.einsum(
            "lshg,lsgk->lshk", gram_matrix, gram_matrix, preferred_element_type=jnp.float32
        )
        poly_term = (quintic_b * gram_matrix.astype(jnp.float32) + quintic_c * square).astype(
            jnp.bfloat16
        )
        product = jnp.einsum(
            "lshg,lsgc->lshc", poly_term, current, preferred_element_type=jnp.float32
        )
        current = (quintic_a * current.astype(jnp.float32) + product).astype(jnp.bfloat16)
    return current


def row_plan(context, cotangent, tile_counts, momentum, weights):
    layers, tok_dev, all_rows = context.shape
    columns = cotangent.shape[2]
    shard_rows = momentum.shape[1]
    position = lax.broadcasted_iota(jnp.int32, (tok_dev, 1), 0)
    live_mask = (position // TILE_TOK < tile_counts[0]).astype(cotangent.dtype)
    masked = cotangent * live_mask[None]
    factor = 1.0 / math.sqrt(tok_dev * lax.axis_size("dp"))

    def layer_term(layer_index):
        block = context[layer_index]
        return (
            lax.dot_general(
                block,
                masked[layer_index],
                (((0,), (0,)), ((), ())),
                preferred_element_type=jnp.float32,
            )
            * factor
        )

    pieces = []
    for layer_index in range(layers):

        def one_term(first_row, row_count, chosen=layer_index):
            return layer_term(chosen)

        pieces.append(
            lax.psum_scatter(
                one_term(jnp.int32(0), lax.axis_size("dp") * shard_rows),
                "dp",
                scatter_dimension=0,
                tiled=True,
            )
        )
    gradient = jnp.stack(pieces)
    moment_new = momentum_rate * momentum + gradient
    nesterov = (gradient + momentum_rate * moment_new).astype(jnp.bfloat16)
    row_start = lax.axis_index("dp") * shard_rows
    slots = min(shard_rows, HEADS_WIN)
    head_ids = (row_start + lax.broadcasted_iota(jnp.int32, (slots,), 0)) % HEADS_WIN
    gathered = lax.all_gather(nesterov, "dp", axis=1, tiled=True)
    grid = gathered.reshape(layers, HEAD, HEADS_WIN, columns)
    slab_block = jnp.transpose(jnp.take(grid, head_ids, axis=2), (0, 2, 1, 3))
    widened = slab_block.astype(jnp.float32)
    sum_squares = lax.psum(jnp.sum(widened * widened, axis=(2, 3)), "mp")
    current = (widened / (jnp.sqrt(sum_squares) + norm_floor)[:, :, None, None]).astype(
        jnp.bfloat16
    )
    orthogonal = quintic(
        current,
        lambda partial_value: lax.psum(partial_value.astype(jnp.bfloat16), "mp").astype(
            jnp.float32
        ),
    )
    local_rows = lax.broadcasted_iota(jnp.int32, (shard_rows,), 0)
    global_rows = row_start + local_rows
    flat_index = local_rows % HEADS_WIN * HEAD + global_rows // HEADS_WIN
    update_rows = jnp.take(
        orthogonal.reshape(layers, slots * HEAD, columns), flat_index, axis=1
    ).astype(jnp.float32)
    update_scale = 0.2 * math.sqrt(max(HEAD, COLS))
    new_weights = weights - learn_rate * (weight_decay * weights + update_scale * update_rows)
    return (moment_new, new_weights)

def dp_index(z, y, c):
    return (z * SIZE_Y + y) * SIZE_C + c


def all_chips():
    return [(z, y, c) for z in range(SIZE_Z) for y in range(SIZE_Y) for c in range(SIZE_C)]


def swap_core(value):
    return lax.ppermute(value, "dp", [(dp_index(z, y, c), dp_index(z, y, 1 - c)) for z, y, c in all_chips()])


def swap_y(value):
    return lax.ppermute(value, "dp", [(dp_index(z, y, c), dp_index(z, 1 - y, c)) for z, y, c in all_chips()])


def swap_x(value):
    return lax.ppermute(value, "mp", [(0, 1), (1, 0)])


def after(value, *earlier):
    return lax.optimization_barrier((value, *earlier))[0]


def contract(left, right, dims):
    return lax.dot_general(left, right, (dims, ((), ())), preferred_element_type=F32)


def ext_kernel(pick, cotangent, momentum, counts, out_ref):
    tokens, rows = cotangent.shape[2], momentum.shape[2]
    position = lax.broadcasted_iota(jnp.int32, (1, tokens), 1)
    live = (position // TILE_TOK < counts[0]).astype(F32)
    out_ref[:, :tokens] = (cotangent[0].astype(F32) * live).astype(BF16)
    mixed_in = mixed_part(momentum[0])
    pad = jnp.zeros((mixed_in.shape[0], HEAD - rows), BF16)
    out_ref[:, tokens:] = jnp.concatenate([mixed_in, pad], axis=1)


def mixed_part(momentum):
    return (momentum * (2.0 * MIX)).astype(BF16)


def slot_kernel(first, second, perm, out_ref):
    tokens = jnp.concatenate([first[...], second[...]], axis=0)
    out_ref[...] = contract(tokens, perm[...], ((1,), (0,))).astype(BF16)


def chunk_kernel(table, ext0, ext1, ext2, ext3, own, near, far, hot, out_ref, *, factor):
    tokens = own.shape[0] // 2
    half = tokens // 2
    low_first = table[SIZE_Z] == 0
    total = contract(ext0[:, :tokens], own[:tokens], ((1,), (0,)))
    total += contract(ext1[:, :tokens], own[tokens:], ((1,), (0,)))
    for source, ext in enumerate((ext2, ext3)):
        here = near[source * half : (source + 1) * half]
        there = far[source * half : (source + 1) * half]
        low = jnp.where(low_first, here, there)
        high = jnp.where(low_first, there, here)
        total += contract(ext[:, :tokens], jnp.concatenate([low, high], axis=0), ((1,), (0,)))
    for source, (left, right) in enumerate(((ext0, ext1), (ext2, ext3))):
        rows = jnp.concatenate([left[:, tokens:], right[:, tokens:]], axis=1)
        total += contract(rows, hot[2 * source : 2 * source + 2].reshape(2 * HEAD, -1), ((1,), (0,)))
    out_ref[0] = total * factor


def gram_kernel(mixed, nesterov_ref, gram_ref, turned_ref):
    value = mixed[...]
    nesterov = (GAIN * value).astype(BF16)
    nesterov_ref[...] = nesterov
    for head in range(2):
        block = nesterov[:, head * HEAD : (head + 1) * HEAD]
        gram_ref[head] = contract(block, block, ((0,), (0,)))
    turned_ref[...] = value.T


def square_dot(left, right):
    return jnp.dot(left, right, precision=lax.Precision.HIGHEST, preferred_element_type=F32)


def ortho_kernel(near, far, nesterov, out_ref):
    row = lax.broadcasted_iota(jnp.int32, (HEAD, HEAD), 0)
    column = lax.broadcasted_iota(jnp.int32, (HEAD, HEAD), 1)
    eye = (row == column).astype(F32)
    for head in range(2):
        raw = near[head] + far[head]
        squares = jnp.sum(raw * eye, axis=(0, 1), keepdims=True)
        scale = 1.0 / (jnp.sqrt(squares) + norm_floor)
        gram = raw * (scale * scale)
        total = None
        for step in range(ITERS):
            poly = quintic_b * gram + quintic_c * square_dot(gram, gram)
            factor = quintic_a * eye + poly
            total = factor if total is None else square_dot(factor, total)
            if step + 1 < ITERS:
                gram = square_dot(square_dot(factor, gram), factor)
        total = total * scale
        high = total.astype(BF16)
        low = (total - high.astype(F32)).astype(BF16)
        block = nesterov[:, head * HEAD : (head + 1) * HEAD]
        out_ref[pl.ds(head * HEAD, HEAD), :] = contract(high, block, ((1,), (1,))) + contract(low, block, ((1,), (1,)))


def final_kernel(mixed_back, ortho_back, order, momentum, weights, momentum_ref, weights_ref, *, update_scale):
    for layer in range(2):
        places = [(z, layer, c) for z in range(SIZE_Z) for c in range(SIZE_C)]
        summed = jnp.concatenate([mixed_back[place] for place in places], axis=0)
        ortho = jnp.concatenate([ortho_back[place] for place in places], axis=0).astype(BF16)
        high = summed.astype(BF16)
        low = (summed - high.astype(F32)).astype(BF16)
        rows = momentum.shape[2]
        mixed = contract(high, order[...], ((0,), (0,))) + contract(low, order[...], ((0,), (0,)))
        update = contract(ortho, order[...], ((0,), (0,)))
        old = momentum[layer]
        gradient = mixed[:, :rows] - 0.5 * mixed_part(old).astype(F32)
        momentum_ref[layer] = momentum_rate * old + gradient
        old = weights[layer]
        weights_ref[layer] = old - learn_rate * (weight_decay * old + update_scale * update[:, :rows])


def vmem_params(**kwargs):
    return pltpu.CompilerParams(vmem_limit_bytes=VMEM_BYTES, **kwargs)


def block_plan(context, cotangent, tile_counts, momentum, weights):
    layers, tok_dev, all_rows = context.shape
    columns = cotangent.shape[2]
    shard_rows = momentum.shape[1]
    depth = shard_rows // HEADS_WIN
    half = tok_dev // 2
    where = lax.axis_index("dp")
    z, y, c = where // (SIZE_Y * SIZE_C), where // SIZE_C % SIZE_Y, where % SIZE_C
    x = lax.axis_index("mp")
    factor = 1.0 / math.sqrt(tok_dev * lax.axis_size("dp"))

    half_send = lax.dynamic_slice(context, (1 - y, x * half, 0), (1, half, all_rows))[0]
    first0 = swap_y(half_send)
    ctx_keep = lax.dynamic_index_in_dim(context, y, 0, False)
    ctx1 = swap_core(ctx_keep)

    cotangent_t = jnp.transpose(cotangent, (0, 2, 1))
    momentum_t = jnp.transpose(momentum, (0, 2, 1))
    weights_t = jnp.transpose(weights, (0, 2, 1))
    wide = tok_dev + HEAD

    def ext_of(layer):
        return pl.pallas_call(
            ext_kernel,
            grid_spec=pltpu.PrefetchScalarGridSpec(
                num_scalar_prefetch=1,
                grid=(1,),
                in_specs=[
                    pl.BlockSpec((1, columns, tok_dev), lambda i, pick: (pick[0], 0, 0)),
                    pl.BlockSpec((1, columns, shard_rows), lambda i, pick: (pick[0], 0, 0)),
                    pl.BlockSpec(memory_space=pltpu.SMEM),
                ],
                out_specs=pl.BlockSpec((columns, wide), lambda i, pick: (0, 0)),
            ),
            out_shape=jax.ShapeDtypeStruct((columns, wide), BF16),
            compiler_params=vmem_params(),
            cost_estimate=pl.CostEstimate(flops=10**6, bytes_accessed=2 * 10**6, transcendentals=0),
        )(layer.reshape(1), cotangent_t, momentum_t, tile_counts)

    ext2 = swap_y(ext_of(1 - y))
    ext_keep = ext_of(y)
    ext1 = swap_core(ext_keep)

    slot_cols = SIZE_Z * 2 * HEAD
    row = lax.broadcasted_iota(jnp.int32, (all_rows, slot_cols), 0)
    col = lax.broadcasted_iota(jnp.int32, (all_rows, slot_cols), 1)
    head = col // (2 * HEAD) * 4 + c * 2 + col // HEAD % 2
    perm = ((row == col % HEAD * HEADS_WIN + head) & (head < HEADS_WIN)).astype(BF16)
    shape = (4, HEAD, slot_cols)
    sender = lax.broadcasted_iota(jnp.int32, shape, 0)
    sender_y = jnp.where(sender // 2 == 0, y, 1 - y)
    sender_c = jnp.where(sender % 2 == 0, c, 1 - c)
    local = lax.broadcasted_iota(jnp.int32, shape, 1)
    col = lax.broadcasted_iota(jnp.int32, shape, 2)
    head = col // (2 * HEAD) * 4 + c * 2 + col // HEAD % 2
    from_row = dp_index(z, sender_y, sender_c) * shard_rows + local
    hit = (from_row == col % HEAD * HEADS_WIN + head) & (head < HEADS_WIN) & (local < shard_rows)
    hot = jnp.where(hit, 0.5 / factor, 0.0).astype(BF16)

    lanes = 2 * HEAD

    def slots_of(first, second):
        tokens = first.shape[0]
        return pl.pallas_call(
            slot_kernel,
            grid=(SIZE_Z,),
            in_specs=[pl.BlockSpec((tokens, all_rows), lambda j: (0, 0))] * 2
            + [pl.BlockSpec((all_rows, lanes), lambda j: (0, j))],
            out_specs=pl.BlockSpec((2 * tokens, lanes), lambda j: (0, j)),
            out_shape=jax.ShapeDtypeStruct((2 * tokens, slot_cols), BF16),
            compiler_params=vmem_params(),
            cost_estimate=pl.CostEstimate(
                flops=4 * tokens * all_rows * slot_cols, bytes_accessed=6 * 10**6, transcendentals=0
            ),
        )(first, second, perm)

    own = slots_of(ctx_keep, ctx1)
    first0 = after(first0, own)
    second0 = swap_x(first0)
    first1 = swap_core(first0)
    near = slots_of(first0, first1)
    second0 = after(second0, near)
    second1 = swap_core(second0)
    ext3 = swap_core(ext2)
    far = slots_of(second0, second1)

    orders = jnp.array([[3, 2, 1, 0], [2, 0, 3, 1], [3, 1, 0, 2], [0, 1, 2, 3]], jnp.int32)
    table = jnp.concatenate([lax.dynamic_index_in_dim(orders, z, 0, False), x.reshape(1)])

    def chunks_of(first):
        full = lambda rows, cols: pl.BlockSpec((rows, cols), lambda j, table: (0, 0))
        part = lambda rows: pl.BlockSpec((rows, lanes), lambda j, table: (0, table[first + j]))
        return pl.pallas_call(
            functools.partial(chunk_kernel, factor=factor),
            grid_spec=pltpu.PrefetchScalarGridSpec(
                num_scalar_prefetch=1,
                grid=(2,),
                in_specs=[full(columns, wide)] * 4
                + [part(2 * tok_dev), part(tok_dev), part(tok_dev)]
                + [pl.BlockSpec((4, HEAD, lanes), lambda j, table: (0, 0, table[first + j]))],
                out_specs=pl.BlockSpec((1, columns, lanes), lambda j, table: (j, 0, 0)),
            ),
            out_shape=jax.ShapeDtypeStruct((2, columns, lanes), F32),
            compiler_params=vmem_params(),
            cost_estimate=pl.CostEstimate(
                flops=4 * columns * (4 * tok_dev + 4 * HEAD) * lanes, bytes_accessed=5 * 10**6, transcendentals=0
            ),
        )(table, ext_keep, ext1, ext2, ext3, own, near, far, hot)

    def along_z(value, pairs):
        pairs = [(dp_index(p, b, a), dp_index(q, b, a)) for p, q in pairs for b in range(SIZE_Y) for a in range(SIZE_C)]
        return lax.ppermute(value.astype(jnp.float16), "dp", pairs)

    early = chunks_of(0)
    up = along_z(early[0], [(0, 1), (1, 2), (2, 3)])
    down = along_z(jnp.where(z == 3, early[0], early[1]), [(3, 2), (2, 1), (1, 0)])
    jump = along_z(early[1], [(0, 2), (3, 1)])
    late = chunks_of(2)
    zero = jnp.zeros((), F32)
    merged = late[0] + jnp.where(z == 1, up.astype(F32), zero) + jnp.where(z == 2, down.astype(F32), zero)
    last = along_z(merged, [(0, 1), (1, 3), (3, 2), (2, 0)])
    mixed = late[1] + jnp.where(z >= 2, up.astype(F32), zero) + jnp.where(z <= 1, down.astype(F32), zero)
    mixed = mixed + jump.astype(F32) + last.astype(F32)

    nesterov, gram, turned = pl.pallas_call(
        gram_kernel,
        out_shape=(
            jax.ShapeDtypeStruct((columns, lanes), BF16),
            jax.ShapeDtypeStruct((2, HEAD, HEAD), F32),
            jax.ShapeDtypeStruct((lanes, columns), F32),
        ),
        compiler_params=vmem_params(),
    )(mixed)
    ortho = pl.pallas_call(
        ortho_kernel,
        out_shape=jax.ShapeDtypeStruct((lanes, columns), F32),
        compiler_params=vmem_params(),
    )(gram, swap_x(gram), nesterov)

    def returned(value):
        value = value.astype(jnp.float16).reshape(2, lax.axis_size("dp"), depth, columns)
        value = jnp.transpose(value, (1, 0, 2, 3)).reshape(-1, 2 * depth, columns)
        value = lax.all_to_all(value, "dp", 0, 0).astype(F32)
        return value.reshape(SIZE_Z, SIZE_Y, SIZE_C, 2 * depth, columns)

    mixed_back = returned(turned)
    ortho_back = returned(ortho)

    count = SIZE_Z * SIZE_C * 2 * depth
    row = lax.broadcasted_iota(jnp.int32, (count, HEAD), 0)
    col = lax.broadcasted_iota(jnp.int32, (count, HEAD), 1)
    order = ((col == row % depth * HEADS_WIN + row // depth) & (row // depth < HEADS_WIN)).astype(BF16)
    out = jax.ShapeDtypeStruct((layers, columns, shard_rows), F32)
    moment_new, new_weights = pl.pallas_call(
        functools.partial(final_kernel, update_scale=0.2 * math.sqrt(max(HEAD, COLS))),
        out_shape=(out, out),
        compiler_params=vmem_params(),
    )(mixed_back, ortho_back, order, momentum_t, weights_t)
    return jnp.transpose(moment_new, (0, 2, 1)), jnp.transpose(new_weights, (0, 2, 1))


def solution(mesh):
    in_specs = (
        P(None, "dp", None),
        P(None, "dp", "mp"),
        P("dp"),
        P(None, "dp", "mp"),
        P(None, "dp", "mp"),
    )
    out_specs = (P(None, "dp", "mp"), P(None, "dp", "mp"))
    small = mesh.shape["dp"] == SIZE_Z * SIZE_Y * SIZE_C and mesh.shape["mp"] == 2
    return jax.shard_map(
        block_plan if small else row_plan, mesh=mesh, in_specs=in_specs, out_specs=out_specs, check_vma=False
    )
```

```python
import functools
import math

import jax
import jax.numpy as jnp
from jax import lax
from jax.experimental import pallas as pl
from jax.experimental.pallas import tpu as pltpu
from jax.sharding import PartitionSpec as P

HEAD = 128
HEADS_WIN = 15
COLS = 1600
ITERS = 3
TILE_TOK = 64


quintic_a = 3.4445
quintic_b = -4.775
quintic_c = 2.0315
momentum_rate = 0.95
learn_rate = 0.02
weight_decay = 0.1
norm_floor = 1e-07

SIZE_Z, SIZE_Y, SIZE_C = 4, 2, 2
GAIN = 1.0 + momentum_rate
MIX = momentum_rate * momentum_rate / GAIN
BF16 = jnp.bfloat16
F32 = jnp.float32
VMEM_BYTES = 20 * 1024 * 1024
COL_PARTS = 1
HALF_PARTS = 1
CHUNK_ORDERS = ((3, 2, 1, 0), (0, 2, 3, 1), (3, 1, 0, 2), (0, 1, 2, 3))
CHUNK_STEPS = len(CHUNK_ORDERS[0])
CHUNK_SENDS = 2
NO_HEAD = -(1 << 20)


def quintic(current, reduce_gram):
    for step_index in range(ITERS):
        partial_value = jnp.einsum(
            "lshc,lsgc->lshg", current, current, preferred_element_type=jnp.float32
        )
        gram_matrix = reduce_gram(partial_value).astype(jnp.bfloat16)
        square = jnp.einsum(
            "lshg,lsgk->lshk", gram_matrix, gram_matrix, preferred_element_type=jnp.float32
        )
        poly_term = (quintic_b * gram_matrix.astype(jnp.float32) + quintic_c * square).astype(
            jnp.bfloat16
        )
        product = jnp.einsum(
            "lshg,lsgc->lshc", poly_term, current, preferred_element_type=jnp.float32
        )
        current = (quintic_a * current.astype(jnp.float32) + product).astype(jnp.bfloat16)
    return current


def row_plan(context, cotangent, tile_counts, momentum, weights):
    layers, tok_dev, all_rows = context.shape
    columns = cotangent.shape[2]
    shard_rows = momentum.shape[1]
    position = lax.broadcasted_iota(jnp.int32, (tok_dev, 1), 0)
    live_mask = (position // TILE_TOK < tile_counts[0]).astype(cotangent.dtype)
    masked = cotangent * live_mask[None]
    factor = 1.0 / math.sqrt(tok_dev * lax.axis_size("dp"))

    def layer_term(layer_index):
        block = context[layer_index]
        return (
            lax.dot_general(
                block,
                masked[layer_index],
                (((0,), (0,)), ((), ())),
                preferred_element_type=jnp.float32,
            )
            * factor
        )

    pieces = []
    for layer_index in range(layers):

        def one_term(first_row, row_count, chosen=layer_index):
            return layer_term(chosen)

        pieces.append(
            lax.psum_scatter(
                one_term(jnp.int32(0), lax.axis_size("dp") * shard_rows),
                "dp",
                scatter_dimension=0,
                tiled=True,
            )
        )
    gradient = jnp.stack(pieces)
    moment_new = momentum_rate * momentum + gradient
    nesterov = (gradient + momentum_rate * moment_new).astype(jnp.bfloat16)
    row_start = lax.axis_index("dp") * shard_rows
    slots = min(shard_rows, HEADS_WIN)
    head_ids = (row_start + lax.broadcasted_iota(jnp.int32, (slots,), 0)) % HEADS_WIN
    gathered = lax.all_gather(nesterov, "dp", axis=1, tiled=True)
    grid = gathered.reshape(layers, HEAD, HEADS_WIN, columns)
    slab_block = jnp.transpose(jnp.take(grid, head_ids, axis=2), (0, 2, 1, 3))
    widened = slab_block.astype(jnp.float32)
    sum_squares = lax.psum(jnp.sum(widened * widened, axis=(2, 3)), "mp")
    current = (widened / (jnp.sqrt(sum_squares) + norm_floor)[:, :, None, None]).astype(
        jnp.bfloat16
    )
    orthogonal = quintic(
        current,
        lambda partial_value: lax.psum(partial_value.astype(jnp.bfloat16), "mp").astype(
            jnp.float32
        ),
    )
    local_rows = lax.broadcasted_iota(jnp.int32, (shard_rows,), 0)
    global_rows = row_start + local_rows
    flat_index = local_rows % HEADS_WIN * HEAD + global_rows // HEADS_WIN
    update_rows = jnp.take(
        orthogonal.reshape(layers, slots * HEAD, columns), flat_index, axis=1
    ).astype(jnp.float32)
    update_scale = 0.2 * math.sqrt(max(HEAD, COLS))
    new_weights = weights - learn_rate * (weight_decay * weights + update_scale * update_rows)
    return (moment_new, new_weights)

def dp_index(z, y, c):
    return (z * SIZE_Y + y) * SIZE_C + c


def all_chips():
    return [(z, y, c) for z in range(SIZE_Z) for y in range(SIZE_Y) for c in range(SIZE_C)]


def swap_core(value):
    return lax.ppermute(value, "dp", [(dp_index(z, y, c), dp_index(z, y, 1 - c)) for z, y, c in all_chips()])


def swap_y(value):
    return lax.ppermute(value, "dp", [(dp_index(z, y, c), dp_index(z, 1 - y, c)) for z, y, c in all_chips()])


def swap_x(value):
    return lax.ppermute(value, "mp", [(0, 1), (1, 0)])


def after(value, *earlier):
    return lax.optimization_barrier((value, *earlier))[0]


def contract(left, right, dims):
    return lax.dot_general(left, right, (dims, ((), ())), preferred_element_type=F32)


def ext_kernel(pick, cotangent, momentum, counts, *out_refs):
    tokens, rows = cotangent.shape[2], momentum.shape[2]
    position = lax.broadcasted_iota(jnp.int32, (1, tokens), 1)
    live = (position // TILE_TOK < counts[0]).astype(F32)
    start = 0
    for out_ref in out_refs:
        part = slice(start, start + out_ref.shape[0])
        start = part.stop
        out_ref[:, :tokens] = (cotangent[0, part].astype(F32) * live).astype(BF16)
        pad = jnp.zeros((out_ref.shape[0], HEAD - rows), BF16)
        out_ref[:, tokens:] = jnp.concatenate([mixed_part(momentum[0, part]), pad], axis=1)


def mixed_part(momentum):
    return (momentum * (2.0 * MIX)).astype(BF16)


def head_of(step, c, index):
    head = step * 4 + c * 2 + index
    return jnp.where(head < HEADS_WIN, head, NO_HEAD)


def slot_kernel(core, *refs):
    *pieces, out_ref, lead = refs
    step = pl.program_id(0)

    @pl.when(step == 0)
    def _():
        row = lax.broadcasted_iota(jnp.int32, lead.shape, 0)
        lead[...] = row - HEADS_WIN * lax.broadcasted_iota(jnp.int32, lead.shape, 1)

    places = [(lead[...] == head_of(step, core[0], index)).astype(F32).astype(BF16) for index in range(2)]
    tokens = jnp.concatenate([piece[...] for piece in pieces], axis=0)
    out_ref[0] = contract(tokens, jnp.concatenate(places, axis=1), ((1,), (0,))).astype(BF16)


def chunk_kernel(table, ext0, ext1, ext2, ext3, own, near, far, send_ref, keep_ref, *, factor, rows):
    step = pl.program_id(0)
    x, z, y, c = (table[CHUNK_STEPS + index] for index in range(4))
    tokens = own.shape[1] // 2
    half = tokens // 2
    low_first = x == 0
    total = contract(ext0[:, :tokens], own[0, :tokens], ((1,), (0,)))
    total += contract(ext1[:, :tokens], own[0, tokens:], ((1,), (0,)))
    for source, ext in enumerate((ext2, ext3)):
        here = near[0, source * half : (source + 1) * half]
        there = far[0, source * half : (source + 1) * half]
        low = jnp.where(low_first, here, there)
        high = jnp.where(low_first, there, here)
        total += contract(ext[:, :tokens], jnp.concatenate([low, high], axis=0), ((1,), (0,)))
    local = lax.broadcasted_iota(jnp.int32, (HEAD, HEAD), 0)
    lead = jnp.where(local < rows, local - HEADS_WIN * lax.broadcasted_iota(jnp.int32, (HEAD, HEAD), 1), 2 * NO_HEAD)
    for sender_y, left, right in ((y, ext0, ext1), (1 - y, ext2, ext3)):
        places = []
        for sender_c in (c, 1 - c):
            first_row = dp_index(z, sender_y, sender_c) * rows
            hits = [lead + first_row == head_of(table[step], c, index) for index in range(2)]
            hits = jnp.concatenate([jnp.where(hit, 0.5 / factor, 0.0) for hit in hits], axis=1)
            places.append(hits.astype(BF16))
        mixed_in = jnp.concatenate([left[:, tokens:], right[:, tokens:]], axis=1)
        total += contract(mixed_in, jnp.concatenate(places, axis=0), ((1,), (0,)))
    total = total * factor

    @pl.when(step < CHUNK_SENDS)
    def _():
        send_ref[0] = total

    @pl.when(step >= CHUNK_SENDS)
    def _():
        keep_ref[0] = total


def gram_kernel(*refs):
    *parts, near_ref, far_ref = refs
    for head in range(2):
        total = None
        for part in parts:
            block = (GAIN * part[:, head * HEAD : (head + 1) * HEAD]).astype(BF16)
            term = contract(block, block, ((0,), (0,)))
            total = term if total is None else total + term
        near_ref[head] = total
        far_ref[head] = total.astype(BF16)


def turn_kernel(*refs):
    *parts, turned_ref, owner_ref = refs
    value = jnp.concatenate([part[...] for part in parts], axis=0).T
    turned_ref[...] = value
    store_by_owner(owner_ref, [value[:HEAD], value[HEAD:]])


def store_by_owner(owner_ref, blocks):
    owners = owner_ref.shape[0]
    depth = HEAD // owners
    for owner in range(owners):
        rows = [block[owner * depth : (owner + 1) * depth] for block in blocks]
        owner_ref[owner] = jnp.concatenate(rows, axis=0).astype(owner_ref.dtype)


def square_dot(left, right):
    return jnp.dot(left, right, precision=lax.Precision.HIGHEST, preferred_element_type=F32)


def ortho_kernel(near, far, turned, out_ref):
    row = lax.broadcasted_iota(jnp.int32, (HEAD, HEAD), 0)
    column = lax.broadcasted_iota(jnp.int32, (HEAD, HEAD), 1)
    eye = (row == column).astype(F32)
    blocks = []
    for head in range(2):
        raw = near[head] + far[head].astype(F32)
        squares = jnp.sum(raw * eye, axis=(0, 1), keepdims=True)
        scale = 1.0 / (jnp.sqrt(squares) + norm_floor)
        gram = raw * (scale * scale)
        total = None
        for step in range(ITERS):
            poly = quintic_b * gram + quintic_c * square_dot(gram, gram)
            factor = quintic_a * eye + poly
            total = factor if total is None else square_dot(factor, total)
            if step + 1 < ITERS:
                gram = square_dot(square_dot(factor, gram), factor)
        total = total * scale
        high = total.astype(BF16)
        low = (total - high.astype(F32)).astype(BF16)
        block = (GAIN * turned[head * HEAD : (head + 1) * HEAD]).astype(BF16)
        blocks.append(contract(high, block, ((1,), (0,))) + contract(low, block, ((1,), (0,))))
    store_by_owner(out_ref, blocks)


def to_rows(back, layer):
    places = [(z, layer, c) for z in range(SIZE_Z) for c in range(SIZE_C)]
    value = jnp.concatenate([back[place] for place in places], axis=0)
    depth = back.shape[3] // 2
    row = lax.broadcasted_iota(jnp.int32, (value.shape[0], HEAD), 0)
    col = lax.broadcasted_iota(jnp.int32, (value.shape[0], HEAD), 1)
    order = (col == row % depth * HEADS_WIN + row // depth) & (row // depth < HEADS_WIN)
    order = order.astype(F32).astype(BF16)
    high = value.astype(BF16)
    result = contract(high, order, ((0,), (0,)))
    if value.dtype == F32:
        result += contract((value - high.astype(F32)).astype(BF16), order, ((0,), (0,)))
    return result


def momentum_kernel(mixed_back, momentum, out_ref):
    for layer in range(2):
        old = momentum[layer]
        gradient = to_rows(mixed_back, layer)[:, : old.shape[1]] - 0.5 * mixed_part(old).astype(F32)
        out_ref[layer] = momentum_rate * old + gradient


def weights_kernel(ortho_back, weights, out_ref, *, update_scale):
    for layer in range(2):
        old = weights[layer]
        update = to_rows(ortho_back, layer)[:, : old.shape[1]]
        out_ref[layer] = old - learn_rate * (weight_decay * old + update_scale * update)


def vmem_params(**kwargs):
    return pltpu.CompilerParams(vmem_limit_bytes=VMEM_BYTES, **kwargs)


def block_plan(context, cotangent, tile_counts, momentum, weights):
    layers, tok_dev, all_rows = context.shape
    columns = cotangent.shape[2]
    shard_rows = momentum.shape[1]
    depth = shard_rows // HEADS_WIN
    half = tok_dev // 2
    where = lax.axis_index("dp")
    z, y, c = where // (SIZE_Y * SIZE_C), where // SIZE_C % SIZE_Y, where % SIZE_C
    x = lax.axis_index("mp")
    factor = 1.0 / math.sqrt(tok_dev * lax.axis_size("dp"))

    size = half // HALF_PARTS
    half_send = [
        lax.dynamic_slice(context, (1 - y, x * half + index * size, 0), (1, size, all_rows))[0]
        for index in range(HALF_PARTS)
    ]
    first0 = [swap_y(piece) for piece in half_send]

    cotangent_t = jnp.transpose(cotangent, (0, 2, 1))
    momentum_t = jnp.transpose(momentum, (0, 2, 1))
    weights_t = jnp.transpose(weights, (0, 2, 1))
    wide = tok_dev + HEAD

    part_cols = [columns // COL_PARTS] * COL_PARTS

    def ext_of(layer):
        return pl.pallas_call(
            ext_kernel,
            grid_spec=pltpu.PrefetchScalarGridSpec(
                num_scalar_prefetch=1,
                grid=(1,),
                in_specs=[
                    pl.BlockSpec((1, columns, tok_dev), lambda i, pick: (pick[0], 0, 0)),
                    pl.BlockSpec((1, columns, shard_rows), lambda i, pick: (pick[0], 0, 0)),
                    pl.BlockSpec(memory_space=pltpu.SMEM),
                ],
                out_specs=[pl.BlockSpec((size, wide), lambda i, pick: (0, 0)) for size in part_cols],
            ),
            out_shape=[jax.ShapeDtypeStruct((size, wide), BF16) for size in part_cols],
            compiler_params=vmem_params(),
            cost_estimate=pl.CostEstimate(flops=10**10, bytes_accessed=2 * 10**6, transcendentals=0),
        )(layer.reshape(1), cotangent_t, momentum_t, tile_counts)

    ext_send = ext_of(after(1 - y, *half_send))
    ext2 = [swap_y(part) for part in ext_send]
    ctx_keep = lax.dynamic_index_in_dim(context, after(y, *half_send), 0, False)
    ctx1 = swap_core(ctx_keep)
    ext_keep = ext_of(after(y, *ext_send))
    ext1 = [swap_core(part) for part in ext_keep]

    lanes = 2 * HEAD

    def slots_of(*pieces, flops):
        tokens = sum(piece.shape[0] for piece in pieces)
        return pl.pallas_call(
            slot_kernel,
            grid_spec=pltpu.PrefetchScalarGridSpec(
                num_scalar_prefetch=1,
                grid=(SIZE_Z,),
                in_specs=[pl.BlockSpec(piece.shape, lambda j, core: (0, 0)) for piece in pieces],
                out_specs=pl.BlockSpec((1, tokens, lanes), lambda j, core: (j, 0, 0)),
                scratch_shapes=[pltpu.VMEM((all_rows, HEAD), jnp.int32)],
            ),
            out_shape=jax.ShapeDtypeStruct((SIZE_Z, tokens, lanes), BF16),
            compiler_params=vmem_params(),
            cost_estimate=pl.CostEstimate(flops=flops, bytes_accessed=10**6, transcendentals=0),
        )(c.reshape(1), *pieces)

    own = slots_of(after(ctx_keep, *ext_send), ctx1, flops=10**6)
    second0, first1 = [], []
    for index in range(HALF_PARTS):
        if index + 1 == HALF_PARTS:
            first0[index] = after(first0[index], own)
        second0.append(swap_x(first0[index]))
        first1.append(swap_core(first0[index]))
    near = slots_of(*first0, *first1, flops=10**10)
    second0 = [after(piece, near) for piece in second0]
    second1 = [swap_core(piece) for piece in second0]
    far = slots_of(*second0, *second1, flops=10**10)
    ext2 = [after(part, near) for part in ext2]
    ext3 = [swap_core(part) for part in ext2]

    table = lax.dynamic_index_in_dim(jnp.array(CHUNK_ORDERS, jnp.int32), z, 0, False)
    table = jnp.concatenate([table, jnp.stack([x, z, y, c])])

    def chunks_of(ext0, ext1, ext2, ext3):
        size = ext0.shape[0]
        full = pl.BlockSpec((size, wide), lambda j, table: (0, 0))
        part = lambda count: pl.BlockSpec((1, count, lanes), lambda j, table: (table[j], 0, 0))
        keeps = CHUNK_STEPS - CHUNK_SENDS
        return pl.pallas_call(
            functools.partial(chunk_kernel, factor=factor, rows=shard_rows),
            grid_spec=pltpu.PrefetchScalarGridSpec(
                num_scalar_prefetch=1,
                grid=(CHUNK_STEPS,),
                in_specs=[full] * 4 + [part(2 * tok_dev), part(tok_dev), part(tok_dev)],
                out_specs=[
                    pl.BlockSpec((1, size, lanes), lambda j, table: (jnp.minimum(j, CHUNK_SENDS - 1), 0, 0)),
                    pl.BlockSpec((1, size, lanes), lambda j, table: (jnp.maximum(j - CHUNK_SENDS, 0), 0, 0)),
                ],
            ),
            out_shape=[
                jax.ShapeDtypeStruct((CHUNK_SENDS, size, lanes), F32),
                jax.ShapeDtypeStruct((keeps, size, lanes), F32),
            ],
            compiler_params=vmem_params(),
            cost_estimate=pl.CostEstimate(
                flops=2 * CHUNK_STEPS * size * (4 * tok_dev + 4 * HEAD) * lanes,
                bytes_accessed=6 * 10**6,
                transcendentals=0,
            ),
        )(table, ext0, ext1, ext2, ext3, own, near, far)

    def along_z(value, pairs):
        pairs = [(dp_index(p, b, a), dp_index(q, b, a)) for p, q in pairs for b in range(SIZE_Y) for a in range(SIZE_C)]
        return lax.ppermute(value.astype(jnp.float16), "dp", pairs)

    def only(condition, value):
        return jnp.where(condition, value.astype(F32), jnp.zeros((), F32))

    arrivals, mixed = [], []
    for part in range(COL_PARTS):
        send, keep = chunks_of(ext_keep[part], ext1[part], ext2[part], ext3[part])
        pair = along_z(send[0], [(0, 1), (1, 0), (2, 3), (3, 2)])
        inner = along_z(send[1], [(1, 2), (2, 1)])
        outer = along_z(send[1], [(0, 2), (3, 1)])
        arrivals.append((keep, pair, inner, outer))
    middle = (z == 1) | (z == 2)
    for keep, pair, inner, outer in arrivals:
        merged = (keep[0] + only(middle, pair)).astype(jnp.float16)
        last = along_z(merged, [(0, 1), (1, 3), (3, 2), (2, 0)])
        base = keep[1] + only(~middle, after(pair, merged)) + (inner.astype(F32) + outer.astype(F32))
        base, last = lax.optimization_barrier((base, last))
        mixed.append(base + last.astype(F32))

    owners = lax.axis_size("dp")
    by_owner = (owners, 2 * depth, columns)
    gram, gram_send = pl.pallas_call(
        gram_kernel,
        out_shape=[jax.ShapeDtypeStruct((2, HEAD, HEAD), kind) for kind in (F32, BF16)],
        compiler_params=vmem_params(),
    )(*mixed)
    gram_far = swap_x(gram_send)
    turned, mixed_send = pl.pallas_call(
        turn_kernel,
        out_shape=[jax.ShapeDtypeStruct((lanes, columns), F32), jax.ShapeDtypeStruct(by_owner, F32)],
        compiler_params=vmem_params(),
        cost_estimate=pl.CostEstimate(flops=10**10, bytes_accessed=2 * 10**6, transcendentals=0),
    )(after(mixed[0], gram), *mixed[1:])
    ortho_send = pl.pallas_call(
        ortho_kernel,
        out_shape=jax.ShapeDtypeStruct(by_owner, BF16),
        compiler_params=vmem_params(),
    )(gram, gram_far, turned)

    def returned(value):
        return lax.all_to_all(value, "dp", 0, 0).reshape(SIZE_Z, SIZE_Y, SIZE_C, 2 * depth, columns)

    out = jax.ShapeDtypeStruct((layers, columns, shard_rows), F32)
    mixed_back = returned(mixed_send.astype(jnp.float16)).astype(F32)
    moment_new = pl.pallas_call(
        momentum_kernel,
        out_shape=out,
        compiler_params=vmem_params(),
        cost_estimate=pl.CostEstimate(flops=10**10, bytes_accessed=2 * 10**6, transcendentals=0),
    )(mixed_back, momentum_t)
    new_weights = pl.pallas_call(
        functools.partial(weights_kernel, update_scale=0.2 * math.sqrt(max(HEAD, COLS))),
        out_shape=out,
        compiler_params=vmem_params(),
    )(returned(ortho_send), weights_t)
    return jnp.transpose(moment_new, (0, 2, 1)), jnp.transpose(new_weights, (0, 2, 1))


def solution(mesh):
    in_specs = (
        P(None, "dp", None),
        P(None, "dp", "mp"),
        P("dp"),
        P(None, "dp", "mp"),
        P(None, "dp", "mp"),
    )
    out_specs = (P(None, "dp", "mp"), P(None, "dp", "mp"))
    small = mesh.shape["dp"] == SIZE_Z * SIZE_Y * SIZE_C and mesh.shape["mp"] == 2
    return jax.shard_map(
        block_plan if small else row_plan, mesh=mesh, in_specs=in_specs, out_specs=out_specs, check_vma=False
    )
```

```python
import functools
import math

import jax
import jax.numpy as jnp
from jax import lax
from jax.experimental import pallas as pl
from jax.experimental.pallas import tpu as pltpu
from jax.sharding import PartitionSpec as P

HEAD = 128
HEADS_WIN = 15
COLS = 1600
ITERS = 3
TILE_TOK = 64


quintic_a = 3.4445
quintic_b = -4.775
quintic_c = 2.0315
momentum_rate = 0.95
learn_rate = 0.02
weight_decay = 0.1
norm_floor = 1e-07

SIZE_Z, SIZE_Y, SIZE_C = 4, 2, 2
GAIN = 1.0 + momentum_rate
MIX = momentum_rate * momentum_rate / GAIN
BF16 = jnp.bfloat16
F32 = jnp.float32
F16 = jnp.float16
VMEM_BYTES = 20 * 1024 * 1024
CHUNK_ORDERS = ((3, 2, 1, 0), (0, 2, 3, 1), (3, 1, 0, 2), (0, 1, 2, 3))
CHUNK_STEPS = len(CHUNK_ORDERS[0])
CHUNK_SENDS = 2
NO_HEAD = -(1 << 20)


def quintic(current, reduce_gram):
    for step_index in range(ITERS):
        partial_value = jnp.einsum(
            "lshc,lsgc->lshg", current, current, preferred_element_type=jnp.float32
        )
        gram_matrix = reduce_gram(partial_value).astype(jnp.bfloat16)
        square = jnp.einsum(
            "lshg,lsgk->lshk", gram_matrix, gram_matrix, preferred_element_type=jnp.float32
        )
        poly_term = (quintic_b * gram_matrix.astype(jnp.float32) + quintic_c * square).astype(
            jnp.bfloat16
        )
        product = jnp.einsum(
            "lshg,lsgc->lshc", poly_term, current, preferred_element_type=jnp.float32
        )
        current = (quintic_a * current.astype(jnp.float32) + product).astype(jnp.bfloat16)
    return current


def row_plan(context, cotangent, tile_counts, momentum, weights):
    layers, tok_dev, all_rows = context.shape
    columns = cotangent.shape[2]
    shard_rows = momentum.shape[1]
    position = lax.broadcasted_iota(jnp.int32, (tok_dev, 1), 0)
    live_mask = (position // TILE_TOK < tile_counts[0]).astype(cotangent.dtype)
    masked = cotangent * live_mask[None]
    factor = 1.0 / math.sqrt(tok_dev * lax.axis_size("dp"))

    def layer_term(layer_index):
        block = context[layer_index]
        return (
            lax.dot_general(
                block,
                masked[layer_index],
                (((0,), (0,)), ((), ())),
                preferred_element_type=jnp.float32,
            )
            * factor
        )

    pieces = []
    for layer_index in range(layers):

        def one_term(first_row, row_count, chosen=layer_index):
            return layer_term(chosen)

        pieces.append(
            lax.psum_scatter(
                one_term(jnp.int32(0), lax.axis_size("dp") * shard_rows),
                "dp",
                scatter_dimension=0,
                tiled=True,
            )
        )
    gradient = jnp.stack(pieces)
    moment_new = momentum_rate * momentum + gradient
    nesterov = (gradient + momentum_rate * moment_new).astype(jnp.bfloat16)
    row_start = lax.axis_index("dp") * shard_rows
    slots = min(shard_rows, HEADS_WIN)
    head_ids = (row_start + lax.broadcasted_iota(jnp.int32, (slots,), 0)) % HEADS_WIN
    gathered = lax.all_gather(nesterov, "dp", axis=1, tiled=True)
    grid = gathered.reshape(layers, HEAD, HEADS_WIN, columns)
    slab_block = jnp.transpose(jnp.take(grid, head_ids, axis=2), (0, 2, 1, 3))
    widened = slab_block.astype(jnp.float32)
    sum_squares = lax.psum(jnp.sum(widened * widened, axis=(2, 3)), "mp")
    current = (widened / (jnp.sqrt(sum_squares) + norm_floor)[:, :, None, None]).astype(
        jnp.bfloat16
    )
    orthogonal = quintic(
        current,
        lambda partial_value: lax.psum(partial_value.astype(jnp.bfloat16), "mp").astype(
            jnp.float32
        ),
    )
    local_rows = lax.broadcasted_iota(jnp.int32, (shard_rows,), 0)
    global_rows = row_start + local_rows
    flat_index = local_rows % HEADS_WIN * HEAD + global_rows // HEADS_WIN
    update_rows = jnp.take(
        orthogonal.reshape(layers, slots * HEAD, columns), flat_index, axis=1
    ).astype(jnp.float32)
    update_scale = 0.2 * math.sqrt(max(HEAD, COLS))
    new_weights = weights - learn_rate * (weight_decay * weights + update_scale * update_rows)
    return (moment_new, new_weights)

def dp_index(z, y, c):
    return (z * SIZE_Y + y) * SIZE_C + c


def all_chips():
    return [(z, y, c) for z in range(SIZE_Z) for y in range(SIZE_Y) for c in range(SIZE_C)]


def swap_core(value):
    return lax.ppermute(value, "dp", [(dp_index(z, y, c), dp_index(z, y, 1 - c)) for z, y, c in all_chips()])


def swap_y(value):
    return lax.ppermute(value, "dp", [(dp_index(z, y, c), dp_index(z, 1 - y, c)) for z, y, c in all_chips()])


def swap_x(value):
    return lax.ppermute(value, "mp", [(0, 1), (1, 0)])


def after(value, *earlier):
    return lax.optimization_barrier((value, *earlier))[0]


def contract(left, right, dims):
    return lax.dot_general(left, right, (dims, ((), ())), preferred_element_type=F32)


def ext_kernel(table, counts, cotangent, momentum, send_ref, keep_ref):
    y = table[CHUNK_STEPS + 2]
    tokens, rows = cotangent.shape[2], momentum.shape[2]
    position = lax.broadcasted_iota(jnp.int32, (1, tokens), 1)
    live = (position // TILE_TOK < counts[0]).astype(F32)
    pad = jnp.zeros((send_ref.shape[0], HEAD - rows), BF16)
    for layer, out_ref in ((1 - y, send_ref), (y, keep_ref)):
        out_ref[:, :tokens] = (cotangent[layer].astype(F32) * live).astype(BF16)
        out_ref[:, tokens:] = jnp.concatenate([mixed_part(momentum[layer]), pad], axis=1)


def mixed_part(momentum):
    return (momentum * (2.0 * MIX)).astype(BF16)


def head_of(step, c, index):
    head = step * 4 + c * 2 + index
    return jnp.where(head < HEADS_WIN, head, NO_HEAD)


def fill_lead(lead):
    row = lax.broadcasted_iota(jnp.int32, lead.shape, 0)
    lead[...] = row - HEADS_WIN * lax.broadcasted_iota(jnp.int32, lead.shape, 1)


def slots(pieces, lead, chunk, c):
    places = [(lead[...] == head_of(chunk, c, index)).astype(F32).astype(BF16) for index in range(2)]
    tokens = jnp.concatenate([piece[...] for piece in pieces], axis=0)
    return contract(tokens, jnp.concatenate(places, axis=1), ((1,), (0,))).astype(BF16)


def momentum_places(table, chunk, sender_y, rows, value):
    z, y, c = (table[CHUNK_STEPS + index] for index in range(1, 4))
    local = lax.broadcasted_iota(jnp.int32, (HEAD, HEAD), 0)
    lead = jnp.where(local < rows, local - HEADS_WIN * lax.broadcasted_iota(jnp.int32, (HEAD, HEAD), 1), 2 * NO_HEAD)
    places = []
    for sender_c in (c, 1 - c):
        first_row = dp_index(z, sender_y, sender_c) * rows
        hits = [lead + first_row == head_of(chunk, c, index) for index in range(2)]
        hits = jnp.concatenate([jnp.where(hit, value, 0.0) for hit in hits], axis=1)
        places.append(hits.astype(BF16))
    return jnp.concatenate(places, axis=0)


def near_kernel(table, first, second, out_ref, lead):
    fill_lead(lead)
    for chunk in range(SIZE_Z):
        out_ref[chunk] = slots((first, second), lead, chunk, table[CHUNK_STEPS + 3])


def own_kernel(table, ctx0, ctx1, ext0, ext1, out_ref, lead, *, factor, rows):
    y, c = table[CHUNK_STEPS + 2], table[CHUNK_STEPS + 3]
    tokens = ctx0.shape[0]
    fill_lead(lead)
    for step in range(CHUNK_STEPS):
        chunk = table[step]
        own = slots((ctx0, ctx1), lead, chunk, c)
        total = contract(ext0[:, :tokens], own[:tokens], ((1,), (0,)))
        total += contract(ext1[:, :tokens], own[tokens:], ((1,), (0,)))
        mixed_in = jnp.concatenate([ext0[:, tokens:], ext1[:, tokens:]], axis=1)
        total += contract(mixed_in, momentum_places(table, chunk, y, rows, 0.5 / factor), ((1,), (0,)))
        out_ref[step] = total


def chunk_kernel(table, ext2, ext3, near, far0, far1, own, send_ref, keep_ref, lead, *, factor, rows):
    x, y, c = table[CHUNK_STEPS], table[CHUNK_STEPS + 2], table[CHUNK_STEPS + 3]
    half = far0.shape[0]
    tokens = 2 * half
    fill_lead(lead)
    for step in range(CHUNK_STEPS):
        chunk = table[step]
        far = slots((far0, far1), lead, chunk, c)
        total = own[step]
        for source, ext in enumerate((ext2, ext3)):
            here = near[chunk, source * half : (source + 1) * half]
            there = far[source * half : (source + 1) * half]
            low = jnp.where(x == 0, here, there)
            high = jnp.where(x == 0, there, here)
            total += contract(ext[:, :tokens], jnp.concatenate([low, high], axis=0), ((1,), (0,)))
        mixed_in = jnp.concatenate([ext2[:, tokens:], ext3[:, tokens:]], axis=1)
        total += contract(mixed_in, momentum_places(table, chunk, 1 - y, rows, 0.5 / factor), ((1,), (0,)))
        if step < CHUNK_SENDS:
            send_ref[step] = total * factor
        else:
            keep_ref[step - CHUNK_SENDS] = total * factor


def gram_kernel(mixed, near_ref, far_ref):
    for head in range(2):
        block = (GAIN * mixed[:, head * HEAD : (head + 1) * HEAD]).astype(BF16)
        total = contract(block, block, ((0,), (0,)))
        near_ref[head] = total
        far_ref[head] = total.astype(BF16)


def turn_kernel(mixed, turned_ref, owner_ref):
    value = mixed[...].T
    turned_ref[...] = value
    store_by_owner(owner_ref, [value[:HEAD], value[HEAD:]])


def store_by_owner(owner_ref, blocks):
    owners = owner_ref.shape[0]
    depth = HEAD // owners
    for owner in range(owners):
        rows = [block[owner * depth : (owner + 1) * depth] for block in blocks]
        owner_ref[owner] = jnp.concatenate(rows, axis=0).astype(owner_ref.dtype)


def square_dot(left, right):
    return jnp.dot(left, right, precision=lax.Precision.HIGHEST, preferred_element_type=F32)


def ortho_kernel(near, far, turned, out_ref):
    row = lax.broadcasted_iota(jnp.int32, (HEAD, HEAD), 0)
    column = lax.broadcasted_iota(jnp.int32, (HEAD, HEAD), 1)
    eye = (row == column).astype(F32)
    heads = range(2)
    raws = [near[head] + far[head].astype(F32) for head in heads]
    scales = [1.0 / (jnp.sqrt(jnp.sum(raw * eye, axis=(0, 1), keepdims=True)) + norm_floor) for raw in raws]
    grams = [raw * (scale * scale) for raw, scale in zip(raws, scales)]
    totals = None
    for step in range(ITERS):
        squares = [square_dot(gram, gram) for gram in grams]
        factors = [quintic_a * eye + quintic_b * gram + quintic_c * square for gram, square in zip(grams, squares)]
        totals = [square_dot(f, t) for f, t in zip(factors, totals)] if totals else factors
        if step + 1 < ITERS:
            grams = [square_dot(f, gram) for f, gram in zip(factors, grams)]
            grams = [square_dot(gram, f) for f, gram in zip(factors, grams)]
    blocks = []
    for head in heads:
        total = totals[head] * scales[head]
        high = total.astype(BF16)
        low = (total - high.astype(F32)).astype(BF16)
        block = (GAIN * turned[head * HEAD : (head + 1) * HEAD]).astype(BF16)
        blocks.append(contract(high, block, ((1,), (0,))) + contract(low, block, ((1,), (0,))))
    store_by_owner(out_ref, blocks)


def to_rows(pieces):
    depth = pieces[0].shape[0] // 2
    value = jnp.concatenate(pieces, axis=0)
    row = lax.broadcasted_iota(jnp.int32, (value.shape[0], HEAD), 0)
    col = lax.broadcasted_iota(jnp.int32, (value.shape[0], HEAD), 1)
    order = (col == row % depth * HEADS_WIN + row // depth) & (row // depth < HEADS_WIN)
    order = order.astype(F32).astype(BF16)
    high = value.astype(BF16)
    result = contract(high, order, ((0,), (0,)))
    if value.dtype == F32:
        result += contract((value - high.astype(F32)).astype(BF16), order, ((0,), (0,)))
    return result


def momentum_kernel(here, mixed_back, momentum, out_ref):
    z, y, c = (here[index] for index in range(3))
    for layer in range(2):
        old = momentum[layer]
        pieces = [
            mixed_back[(y ^ layer) * SIZE_C + (c ^ core), z ^ chip] for chip in range(SIZE_Z) for core in range(SIZE_C)
        ]
        gradient = to_rows(pieces)[:, : old.shape[1]] - 0.5 * mixed_part(old).astype(F32)
        out_ref[layer] = momentum_rate * old + gradient


def weights_kernel(ortho_back, weights, out_ref, *, update_scale):
    for layer in range(2):
        old = weights[layer]
        pieces = [ortho_back[chip, layer, core] for chip in range(SIZE_Z) for core in range(SIZE_C)]
        update = to_rows(pieces)[:, : old.shape[1]]
        out_ref[layer] = old - learn_rate * (weight_decay * old + update_scale * update)


def vmem_params(**kwargs):
    return pltpu.CompilerParams(vmem_limit_bytes=VMEM_BYTES, **kwargs)


def block_plan(context, cotangent, tile_counts, momentum, weights):
    layers, tok_dev, all_rows = context.shape
    columns = cotangent.shape[2]
    shard_rows = momentum.shape[1]
    depth = shard_rows // HEADS_WIN
    half = tok_dev // 2
    where = lax.axis_index("dp")
    z, y, c = where // (SIZE_Y * SIZE_C), where // SIZE_C % SIZE_Y, where % SIZE_C
    x = lax.axis_index("mp")
    factor = 1.0 / math.sqrt(tok_dev * lax.axis_size("dp"))

    half_send = lax.dynamic_slice(context, (1 - y, x * half, 0), (1, half, all_rows))[0]
    first0 = swap_y(half_send)

    cotangent_t = jnp.transpose(cotangent, (0, 2, 1))
    momentum_t = jnp.transpose(momentum, (0, 2, 1))
    weights_t = jnp.transpose(weights, (0, 2, 1))
    wide = tok_dev + HEAD

    table = lax.dynamic_index_in_dim(jnp.array(CHUNK_ORDERS, jnp.int32), z, 0, False)
    table = jnp.concatenate([table, jnp.stack([x, z, y, c])])
    smem, vmem = pl.BlockSpec(memory_space=pltpu.SMEM), pl.BlockSpec(memory_space=pltpu.VMEM)
    ext_send, ext_keep = pl.pallas_call(
        ext_kernel,
        in_specs=[smem, smem, vmem, vmem],
        out_shape=[jax.ShapeDtypeStruct((columns, wide), BF16)] * 2,
        compiler_params=vmem_params(),
        cost_estimate=pl.CostEstimate(flops=10**10, bytes_accessed=2 * 10**6, transcendentals=0),
    )(after(table, half_send), tile_counts, cotangent_t, momentum_t)
    ext2 = swap_y(ext_send)
    ctx_keep = lax.dynamic_index_in_dim(context, after(y, half_send), 0, False)
    ctx1 = swap_core(ctx_keep)
    ext1 = swap_core(ext_keep)

    lanes = 2 * HEAD

    def planned(kernel, out_shape, *args):
        return pl.pallas_call(
            kernel,
            in_specs=[smem] + [vmem] * len(args),
            out_shape=out_shape,
            scratch_shapes=[pltpu.VMEM((all_rows, HEAD), jnp.int32)],
            compiler_params=vmem_params(),
            cost_estimate=pl.CostEstimate(flops=10**3, bytes_accessed=10**3, transcendentals=0),
        )(table, *args)

    def chunks(count):
        return jax.ShapeDtypeStruct((count, columns, lanes), F32)

    first0 = after(first0, ext_keep, table)
    second0 = swap_x(first0)
    first1 = swap_core(first0)
    own = planned(
        functools.partial(own_kernel, factor=factor, rows=shard_rows),
        chunks(CHUNK_STEPS),
        after(ctx_keep, first0),
        ctx1,
        ext_keep,
        ext1,
    )
    near = planned(near_kernel, jax.ShapeDtypeStruct((SIZE_Z, tok_dev, lanes), BF16), first0, first1)
    second0 = after(second0, near, own)
    second1 = swap_core(second0)
    ext2 = after(ext2, near, own)
    ext3 = swap_core(ext2)
    send, keep = planned(
        functools.partial(chunk_kernel, factor=factor, rows=shard_rows),
        [chunks(CHUNK_SENDS), chunks(CHUNK_STEPS - CHUNK_SENDS)],
        ext2,
        ext3,
        near,
        second0,
        second1,
        own,
    )

    def along_z(value, pairs):
        pairs = [(dp_index(p, b, a), dp_index(q, b, a)) for p, q in pairs for b in range(SIZE_Y) for a in range(SIZE_C)]
        return lax.ppermute(value, "dp", pairs)

    def only(condition, value):
        return jnp.where(condition, value.astype(F32), jnp.zeros((), F32))

    sent = send.astype(F16)
    pair = along_z(sent[0], [(0, 1), (1, 0), (2, 3), (3, 2)])
    inner = along_z(sent[1], [(1, 2), (2, 1)])
    outer = along_z(sent[1], [(0, 2), (3, 1)])
    middle = (z == 1) | (z == 2)
    merged = (keep[0] + only(middle, pair)).astype(F16)
    last = along_z(merged, [(0, 1), (1, 3), (3, 2), (2, 0)])
    base = keep[1] + only(~middle, after(pair, merged)) + (outer.astype(F32) + inner.astype(F32))
    base, last = lax.optimization_barrier((base, last))
    mixed = base + last.astype(F32)

    owners = lax.axis_size("dp")
    by_owner = (owners, 2 * depth, columns)
    gram, gram_send = pl.pallas_call(
        gram_kernel,
        out_shape=[jax.ShapeDtypeStruct((2, HEAD, HEAD), kind) for kind in (F32, BF16)],
        compiler_params=vmem_params(),
    )(mixed)
    gram_far = swap_x(gram_send)
    turned, mixed_send = pl.pallas_call(
        turn_kernel,
        out_shape=[jax.ShapeDtypeStruct((lanes, columns), F32), jax.ShapeDtypeStruct(by_owner, F32)],
        compiler_params=vmem_params(),
        cost_estimate=pl.CostEstimate(flops=10**10, bytes_accessed=2 * 10**6, transcendentals=0),
    )(after(mixed, gram))
    ortho_send = pl.pallas_call(
        ortho_kernel,
        out_shape=jax.ShapeDtypeStruct(by_owner, BF16),
        compiler_params=vmem_params(),
    )(gram, gram_far, turned)

    mixed_send = mixed_send.astype(F16).reshape(SIZE_Z, SIZE_Y * SIZE_C, 2 * depth, columns)
    arrived = []
    for apart in range(SIZE_Z):
        piece = lax.dynamic_index_in_dim(mixed_send, z ^ apart, 0, False)
        arrived.append(along_z(piece, [(k, k ^ apart) for k in range(SIZE_Z)]) if apart else piece)
    mixed_back = []
    for apart in range(SIZE_Y * SIZE_C):
        mine = (y * SIZE_C + c) ^ apart
        piece = jnp.stack([lax.dynamic_index_in_dim(value, mine, 0, False) for value in arrived])
        if apart:
            piece = lax.ppermute(piece, "dp", [(k, k ^ apart) for k in range(owners)])
        mixed_back.append(piece)
    mixed_back = jnp.stack(mixed_back).astype(F32)

    out = jax.ShapeDtypeStruct((layers, columns, shard_rows), F32)
    moment_new = pl.pallas_call(
        momentum_kernel,
        in_specs=[smem, vmem, vmem],
        out_shape=out,
        compiler_params=vmem_params(),
        cost_estimate=pl.CostEstimate(flops=10**10, bytes_accessed=2 * 10**6, transcendentals=0),
    )(jnp.stack([z, y, c]), mixed_back, momentum_t)
    ortho_back = lax.all_to_all(ortho_send, "dp", 0, 0).reshape(SIZE_Z, SIZE_Y, SIZE_C, 2 * depth, columns)
    new_weights = pl.pallas_call(
        functools.partial(weights_kernel, update_scale=0.2 * math.sqrt(max(HEAD, COLS))),
        out_shape=out,
        compiler_params=vmem_params(),
    )(ortho_back, weights_t)
    return jnp.transpose(moment_new, (0, 2, 1)), jnp.transpose(new_weights, (0, 2, 1))


def solution(mesh):
    in_specs = (
        P(None, "dp", None),
        P(None, "dp", "mp"),
        P("dp"),
        P(None, "dp", "mp"),
        P(None, "dp", "mp"),
    )
    out_specs = (P(None, "dp", "mp"), P(None, "dp", "mp"))
    small = mesh.shape["dp"] == SIZE_Z * SIZE_Y * SIZE_C and mesh.shape["mp"] == 2
    return jax.shard_map(
        block_plan if small else row_plan, mesh=mesh, in_specs=in_specs, out_specs=out_specs, check_vma=False
    )
```

```python
import functools
import math

import jax
import jax.numpy as jnp
from jax import lax
from jax.experimental import pallas as pl
from jax.experimental.pallas import tpu as pltpu
from jax.sharding import PartitionSpec as P

HEAD = 128
HEADS_WIN = 15
COLS = 1600
ITERS = 3
TILE_TOK = 64


quintic_a = 3.4445
quintic_b = -4.775
quintic_c = 2.0315
momentum_rate = 0.95
learn_rate = 0.02
weight_decay = 0.1
norm_floor = 1e-07

SIZE_Z, SIZE_Y, SIZE_C = 4, 2, 2
GAIN = 1.0 + momentum_rate
MIX = momentum_rate * momentum_rate / GAIN
BF16 = jnp.bfloat16
F32 = jnp.float32
F16 = jnp.float16
VMEM_BYTES = 20 * 1024 * 1024
CHUNK_ORDERS = ((3, 2, 1, 0), (0, 2, 3, 1), (3, 1, 0, 2), (0, 1, 2, 3))
CHUNK_STEPS = len(CHUNK_ORDERS[0])
CHUNK_SENDS = 2
NO_HEAD = -(1 << 20)
HALF_HEAD = HEAD // 2


def quintic(current, reduce_gram):
    for step_index in range(ITERS):
        partial_value = jnp.einsum(
            "lshc,lsgc->lshg", current, current, preferred_element_type=jnp.float32
        )
        gram_matrix = reduce_gram(partial_value).astype(jnp.bfloat16)
        square = jnp.einsum(
            "lshg,lsgk->lshk", gram_matrix, gram_matrix, preferred_element_type=jnp.float32
        )
        poly_term = (quintic_b * gram_matrix.astype(jnp.float32) + quintic_c * square).astype(
            jnp.bfloat16
        )
        product = jnp.einsum(
            "lshg,lsgc->lshc", poly_term, current, preferred_element_type=jnp.float32
        )
        current = (quintic_a * current.astype(jnp.float32) + product).astype(jnp.bfloat16)
    return current


def row_plan(context, cotangent, tile_counts, momentum, weights):
    layers, tok_dev, all_rows = context.shape
    columns = cotangent.shape[2]
    shard_rows = momentum.shape[1]
    position = lax.broadcasted_iota(jnp.int32, (tok_dev, 1), 0)
    live_mask = (position // TILE_TOK < tile_counts[0]).astype(cotangent.dtype)
    masked = cotangent * live_mask[None]
    factor = 1.0 / math.sqrt(tok_dev * lax.axis_size("dp"))

    def layer_term(layer_index):
        block = context[layer_index]
        return (
            lax.dot_general(
                block,
                masked[layer_index],
                (((0,), (0,)), ((), ())),
                preferred_element_type=jnp.float32,
            )
            * factor
        )

    pieces = []
    for layer_index in range(layers):

        def one_term(first_row, row_count, chosen=layer_index):
            return layer_term(chosen)

        pieces.append(
            lax.psum_scatter(
                one_term(jnp.int32(0), lax.axis_size("dp") * shard_rows),
                "dp",
                scatter_dimension=0,
                tiled=True,
            )
        )
    gradient = jnp.stack(pieces)
    moment_new = momentum_rate * momentum + gradient
    nesterov = (gradient + momentum_rate * moment_new).astype(jnp.bfloat16)
    row_start = lax.axis_index("dp") * shard_rows
    slots = min(shard_rows, HEADS_WIN)
    head_ids = (row_start + lax.broadcasted_iota(jnp.int32, (slots,), 0)) % HEADS_WIN
    gathered = lax.all_gather(nesterov, "dp", axis=1, tiled=True)
    grid = gathered.reshape(layers, HEAD, HEADS_WIN, columns)
    slab_block = jnp.transpose(jnp.take(grid, head_ids, axis=2), (0, 2, 1, 3))
    widened = slab_block.astype(jnp.float32)
    sum_squares = lax.psum(jnp.sum(widened * widened, axis=(2, 3)), "mp")
    current = (widened / (jnp.sqrt(sum_squares) + norm_floor)[:, :, None, None]).astype(
        jnp.bfloat16
    )
    orthogonal = quintic(
        current,
        lambda partial_value: lax.psum(partial_value.astype(jnp.bfloat16), "mp").astype(
            jnp.float32
        ),
    )
    local_rows = lax.broadcasted_iota(jnp.int32, (shard_rows,), 0)
    global_rows = row_start + local_rows
    flat_index = local_rows % HEADS_WIN * HEAD + global_rows // HEADS_WIN
    update_rows = jnp.take(
        orthogonal.reshape(layers, slots * HEAD, columns), flat_index, axis=1
    ).astype(jnp.float32)
    update_scale = 0.2 * math.sqrt(max(HEAD, COLS))
    new_weights = weights - learn_rate * (weight_decay * weights + update_scale * update_rows)
    return (moment_new, new_weights)

def dp_index(z, y, c):
    return (z * SIZE_Y + y) * SIZE_C + c


def all_chips():
    return [(z, y, c) for z in range(SIZE_Z) for y in range(SIZE_Y) for c in range(SIZE_C)]


def swap_core(value):
    return lax.ppermute(value, "dp", [(dp_index(z, y, c), dp_index(z, y, 1 - c)) for z, y, c in all_chips()])


def swap_y(value):
    return lax.ppermute(value, "dp", [(dp_index(z, y, c), dp_index(z, 1 - y, c)) for z, y, c in all_chips()])


def swap_x(value):
    return lax.ppermute(value, "mp", [(0, 1), (1, 0)])


def after(value, *earlier):
    return lax.optimization_barrier((value, *earlier))[0]


def contract(left, right, dims):
    return lax.dot_general(left, right, (dims, ((), ())), preferred_element_type=F32)


def ext_kernel(table, counts, cotangent, momentum, send_ref, keep_ref):
    y = table[CHUNK_STEPS + 2]
    tokens, rows = cotangent.shape[2], momentum.shape[2]
    position = lax.broadcasted_iota(jnp.int32, (1, tokens), 1)
    live = (position // TILE_TOK < counts[0]).astype(F32)
    pad = jnp.zeros((send_ref.shape[0], HEAD - rows), BF16)
    for layer, out_ref in ((1 - y, send_ref), (y, keep_ref)):
        out_ref[:, :tokens] = (cotangent[layer].astype(F32) * live).astype(BF16)
        out_ref[:, tokens:] = jnp.concatenate([mixed_part(momentum[layer]), pad], axis=1)


def mixed_part(momentum):
    return (momentum * (2.0 * MIX)).astype(BF16)


def lane_lead(rows):
    row = lax.broadcasted_iota(jnp.int32, (rows, HEAD), 0)
    lane = lax.broadcasted_iota(jnp.int32, (rows, HEAD), 1)
    return row - HEADS_WIN * (lane % HALF_HEAD) - lane // HALF_HEAD


def slot_hits(lead, shift, chunk, c):
    first = chunk * 4 + c * 2
    lane = lax.broadcasted_iota(jnp.int32, lead.shape, 1)
    return (lead == first + shift) & (lane < jnp.where(first + 1 < HEADS_WIN, HEAD, HALF_HEAD))


def fill_slots(pieces, lead, table, refs, steps=range(CHUNK_STEPS)):
    lead[...] = lane_lead(lead.shape[0])
    window, columns = lead.shape[0], pieces[0].shape[-1]
    tokens = jnp.concatenate([piece[...] for piece in pieces], axis=0)
    for pair in steps[::2]:
        for half in range(2):
            first = half * (columns - window)
            shift = half * (columns // 2) - first
            places = [
                slot_hits(lead[...], shift, table[pair + index], table[CHUNK_STEPS + 3]).astype(F32).astype(BF16)
                for index in range(2)
            ]
            moved = contract(tokens[:, first : first + window], jnp.concatenate(places, axis=1), ((1,), (0,)))
            moved = moved.astype(BF16)
            for index in range(2):
                row = 0
                for ref in refs:
                    count = ref.shape[1]
                    ref[pair - steps[0] + index, :, half * HEAD : (half + 1) * HEAD] = moved[
                        row : row + count, index * HEAD : (index + 1) * HEAD
                    ]
                    row += count


def momentum_places(table, chunk, sender_y, rows, value):
    z, y, c = (table[CHUNK_STEPS + index] for index in range(1, 4))
    local = lax.broadcasted_iota(jnp.int32, (HEAD, HEAD), 0)
    lead = jnp.where(local < rows, lane_lead(HEAD), NO_HEAD)
    places = []
    for sender_c in (c, 1 - c):
        first_row = dp_index(z, sender_y, sender_c) * rows
        hits = [slot_hits(lead + first_row, half * HALF_HEAD * HEADS_WIN, chunk, c) for half in range(2)]
        hits = jnp.concatenate([jnp.where(hit, value, 0.0) for hit in hits], axis=1)
        places.append(hits.astype(BF16))
    return jnp.concatenate(places, axis=0)


def near_kernel(table, first, second, out_ref, lead):
    fill_slots((first, second), lead, table, (out_ref,))


def chip_part(ext0, ext1, tokens, places):
    count = tokens.shape[0] // 2
    total = contract(ext0[:, :count], tokens[:count], ((1,), (0,)))
    total += contract(ext1[:, :count], tokens[count:], ((1,), (0,)))
    mixed_in = jnp.concatenate([ext0[:, count:], ext1[:, count:]], axis=1)
    return total + contract(mixed_in, places, ((1,), (0,)))


def own_kernel(table, ctx0, ctx1, ext0, ext1, out_ref, lead, own, *, factor, rows):
    fill_slots((ctx0, ctx1), lead, table, (own,))
    for step in range(CHUNK_STEPS):
        places = momentum_places(table, table[step], table[CHUNK_STEPS + 2], rows, 0.5 / factor)
        out_ref[step] = chip_part(ext0[...], ext1[...], own[step], places)


def chunk_kernel(table, ext2, ext3, near, far0, far1, own, *refs, factor, rows, steps):
    *out_refs, lead, far = refs
    x, y = table[CHUNK_STEPS], table[CHUNK_STEPS + 2]
    half = far0.shape[0]
    tokens = 2 * half
    fill_slots((far0, far1), lead, table, (far,), steps)
    for step, out_ref in zip(steps, out_refs):
        total = own[step]
        for source, ext in enumerate((ext2, ext3)):
            here = near[step, source * half : (source + 1) * half]
            there = far[step - steps[0], source * half : (source + 1) * half]
            low = jnp.where(x == 0, here, there)
            high = jnp.where(x == 0, there, here)
            total += contract(ext[:, :tokens], jnp.concatenate([low, high], axis=0), ((1,), (0,)))
        mixed_in = jnp.concatenate([ext2[:, tokens:], ext3[:, tokens:]], axis=1)
        total += contract(mixed_in, momentum_places(table, table[step], 1 - y, rows, 0.5 / factor), ((1,), (0,)))
        out_ref[...] = total * factor


def head_rows(value, head):
    first, second = (value[start : start + HALF_HEAD] for start in (head * HALF_HEAD, HEAD + head * HALF_HEAD))
    return jnp.concatenate([first, second], axis=0)


def gram_kernel(mixed, near_ref, far_ref):
    block = (GAIN * mixed[...]).astype(BF16)
    total = contract(block, block, ((0,), (0,)))
    for head in range(2):
        gram = head_rows(head_rows(total, head).T, head)
        near_ref[head] = gram
        far_ref[head] = gram.astype(BF16)


def turn_kernel(mixed, turned_ref, owner_ref):
    value = mixed[...].T
    blocks = [head_rows(value, head) for head in range(2)]
    for head in range(2):
        turned_ref[head * HEAD : (head + 1) * HEAD] = blocks[head]
    store_by_owner(owner_ref, blocks)


def store_by_owner(owner_ref, blocks):
    owners = owner_ref.shape[0]
    depth = HEAD // owners
    for owner in range(owners):
        rows = [block[owner * depth : (owner + 1) * depth] for block in blocks]
        owner_ref[owner] = jnp.concatenate(rows, axis=0).astype(owner_ref.dtype)


def square_dot(left, right):
    return jnp.dot(left, right, precision=lax.Precision.HIGHEST, preferred_element_type=F32)


def ortho_kernel(near, far, turned, out_ref):
    row = lax.broadcasted_iota(jnp.int32, (HEAD, HEAD), 0)
    column = lax.broadcasted_iota(jnp.int32, (HEAD, HEAD), 1)
    eye = (row == column).astype(F32)
    heads = range(2)
    raws = [near[head] + far[head].astype(F32) for head in heads]
    scales = [1.0 / (jnp.sqrt(jnp.sum(raw * eye, axis=(0, 1), keepdims=True)) + norm_floor) for raw in raws]
    grams = [raw * (scale * scale) for raw, scale in zip(raws, scales)]
    totals = None
    for step in range(ITERS):
        squares = [square_dot(gram, gram) for gram in grams]
        factors = [quintic_a * eye + quintic_b * gram + quintic_c * square for gram, square in zip(grams, squares)]
        totals = [square_dot(f, t) for f, t in zip(factors, totals)] if totals else factors
        if step + 1 < ITERS:
            grams = [square_dot(f, gram) for f, gram in zip(factors, grams)]
            grams = [square_dot(gram, f) for f, gram in zip(factors, grams)]
    blocks = []
    for head in heads:
        total = totals[head] * scales[head]
        high = total.astype(BF16)
        low = (total - high.astype(F32)).astype(BF16)
        block = (GAIN * turned[head * HEAD : (head + 1) * HEAD]).astype(BF16)
        blocks.append(contract(high, block, ((1,), (0,))) + contract(low, block, ((1,), (0,))))
    store_by_owner(out_ref, blocks)


def to_rows(pieces):
    depth = pieces[0].shape[0] // 2
    value = jnp.concatenate(pieces, axis=0)
    row = lax.broadcasted_iota(jnp.int32, (value.shape[0], HEAD), 0)
    col = lax.broadcasted_iota(jnp.int32, (value.shape[0], HEAD), 1)
    order = (col == row % depth * HEADS_WIN + row // depth) & (row // depth < HEADS_WIN)
    order = order.astype(F32).astype(BF16)
    high = value.astype(BF16)
    result = contract(high, order, ((0,), (0,)))
    if value.dtype == F32:
        result += contract((value - high.astype(F32)).astype(BF16), order, ((0,), (0,)))
    return result


def momentum_kernel(here, mixed_back, momentum, out_ref):
    z, y, c = (here[index] for index in range(3))
    for layer in range(2):
        old = momentum[layer]
        pieces = [
            mixed_back[(y ^ layer) * SIZE_C + (c ^ core), z ^ chip] for chip in range(SIZE_Z) for core in range(SIZE_C)
        ]
        gradient = to_rows(pieces)[:, : old.shape[1]] - 0.5 * mixed_part(old).astype(F32)
        out_ref[layer] = momentum_rate * old + gradient


def weights_kernel(ortho_back, weights, out_ref, *, update_scale):
    for layer in range(2):
        old = weights[layer]
        pieces = [ortho_back[chip, layer, core] for chip in range(SIZE_Z) for core in range(SIZE_C)]
        update = to_rows(pieces)[:, : old.shape[1]]
        out_ref[layer] = old - learn_rate * (weight_decay * old + update_scale * update)


def vmem_params(**kwargs):
    return pltpu.CompilerParams(vmem_limit_bytes=VMEM_BYTES, **kwargs)


def block_plan(context, cotangent, tile_counts, momentum, weights):
    layers, tok_dev, all_rows = context.shape
    columns = cotangent.shape[2]
    shard_rows = momentum.shape[1]
    depth = shard_rows // HEADS_WIN
    half = tok_dev // 2
    where = lax.axis_index("dp")
    z, y, c = where // (SIZE_Y * SIZE_C), where // SIZE_C % SIZE_Y, where % SIZE_C
    x = lax.axis_index("mp")
    factor = 1.0 / math.sqrt(tok_dev * lax.axis_size("dp"))

    half_send = lax.dynamic_slice(context, (1 - y, x * half, 0), (1, half, all_rows))[0]
    first0 = swap_y(half_send)

    cotangent_t = jnp.transpose(cotangent, (0, 2, 1))
    momentum_t = jnp.transpose(momentum, (0, 2, 1))
    weights_t = jnp.transpose(weights, (0, 2, 1))
    wide = tok_dev + HEAD

    table = lax.dynamic_index_in_dim(jnp.array(CHUNK_ORDERS, jnp.int32), z, 0, False)
    table = jnp.concatenate([table, jnp.stack([x, z, y, c])])
    smem, vmem = pl.BlockSpec(memory_space=pltpu.SMEM), pl.BlockSpec(memory_space=pltpu.VMEM)
    ext_send, ext_keep = pl.pallas_call(
        ext_kernel,
        in_specs=[smem, smem, vmem, vmem],
        out_shape=[jax.ShapeDtypeStruct((columns, wide), BF16)] * 2,
        compiler_params=vmem_params(),
        cost_estimate=pl.CostEstimate(flops=10**10, bytes_accessed=2 * 10**6, transcendentals=0),
    )(after(table, half_send), tile_counts, cotangent_t, momentum_t)
    ext2 = swap_y(ext_send)
    ctx_keep = lax.dynamic_index_in_dim(context, after(y, half_send), 0, False)
    ctx1 = swap_core(ctx_keep)
    ext1 = swap_core(ext_keep)

    lanes = 2 * HEAD

    window = -(-all_rows // 2 // HEAD) * HEAD

    def planned(kernel, out_shape, *args, tokens):
        scratch = [pltpu.VMEM((window, HEAD), jnp.int32)]
        if tokens:
            scratch.append(pltpu.VMEM((CHUNK_STEPS, tokens, lanes), BF16))
        return pl.pallas_call(
            kernel,
            in_specs=[smem] + [vmem] * len(args),
            out_shape=out_shape,
            scratch_shapes=scratch,
            compiler_params=vmem_params(),
            cost_estimate=pl.CostEstimate(flops=10**3, bytes_accessed=10**3, transcendentals=0),
        )(table, *args)

    def chunks(count):
        return jax.ShapeDtypeStruct((count, columns, lanes), F32)

    first0 = after(first0, ext_keep, table)
    second0 = swap_x(first0)
    first1 = swap_core(first0)
    own = planned(
        functools.partial(own_kernel, factor=factor, rows=shard_rows),
        chunks(CHUNK_STEPS),
        after(ctx_keep, first0),
        ctx1,
        ext_keep,
        ext1,
        tokens=2 * tok_dev,
    )
    near = planned(near_kernel, jax.ShapeDtypeStruct((CHUNK_STEPS, tok_dev, lanes), BF16), first0, first1, tokens=0)
    second0 = after(second0, near, own)
    second1 = swap_core(second0)
    ext2 = after(ext2, near, own)
    ext3 = swap_core(ext2)
    one = jax.ShapeDtypeStruct((columns, lanes), F32)
    chunk = [
        planned(
            functools.partial(chunk_kernel, factor=factor, rows=shard_rows, steps=steps),
            [one] * len(steps),
            ext2,
            ext3,
            near,
            second0,
            second1,
            own,
            tokens=tok_dev,
        )
        for steps in (range(CHUNK_SENDS), range(CHUNK_SENDS, CHUNK_STEPS))
    ]
    chunk = [*chunk[0], *chunk[1]]

    def along_z(value, pairs):
        pairs = [(dp_index(p, b, a), dp_index(q, b, a)) for p, q in pairs for b in range(SIZE_Y) for a in range(SIZE_C)]
        return lax.ppermute(value, "dp", pairs)

    def only(condition, value):
        return jnp.where(condition, value.astype(F32), jnp.zeros((), F32))

    sent = [value.astype(F16) for value in chunk[:CHUNK_SENDS]]
    pair = along_z(sent[0], [(0, 1), (1, 0), (2, 3), (3, 2)])
    inner = along_z(sent[1], [(1, 2), (2, 1)])
    outer = along_z(sent[1], [(0, 2), (3, 1)])
    middle = (z == 1) | (z == 2)
    merged = (chunk[2] + only(middle, pair)).astype(F16)
    last = along_z(merged, [(0, 1), (1, 3), (3, 2), (2, 0)])
    base = chunk[3] + only(~middle, after(pair, merged)) + (outer.astype(F32) + inner.astype(F32))
    base, last = lax.optimization_barrier((base, last))
    mixed = base + last.astype(F32)

    owners = lax.axis_size("dp")
    by_owner = (owners, 2 * depth, columns)
    gram, gram_send = pl.pallas_call(
        gram_kernel,
        out_shape=[jax.ShapeDtypeStruct((2, HEAD, HEAD), kind) for kind in (F32, BF16)],
        compiler_params=vmem_params(),
    )(mixed)
    gram_far = swap_x(gram_send)
    turned, mixed_send = pl.pallas_call(
        turn_kernel,
        out_shape=[jax.ShapeDtypeStruct((lanes, columns), F32), jax.ShapeDtypeStruct(by_owner, F32)],
        compiler_params=vmem_params(),
        cost_estimate=pl.CostEstimate(flops=10**10, bytes_accessed=2 * 10**6, transcendentals=0),
    )(after(mixed, gram))
    ortho_send = pl.pallas_call(
        ortho_kernel,
        out_shape=jax.ShapeDtypeStruct(by_owner, BF16),
        compiler_params=vmem_params(),
    )(gram, gram_far, turned)

    mixed_send = mixed_send.astype(F16).reshape(SIZE_Z, SIZE_Y * SIZE_C, 2 * depth, columns)
    arrived = []
    for apart in range(SIZE_Z):
        piece = lax.dynamic_index_in_dim(mixed_send, z ^ apart, 0, False)
        arrived.append(along_z(piece, [(k, k ^ apart) for k in range(SIZE_Z)]) if apart else piece)
    mixed_back = []
    for apart in range(SIZE_Y * SIZE_C):
        mine = (y * SIZE_C + c) ^ apart
        piece = jnp.stack([lax.dynamic_index_in_dim(value, mine, 0, False) for value in arrived])
        if apart:
            piece = lax.ppermute(piece, "dp", [(k, k ^ apart) for k in range(owners)])
        mixed_back.append(piece)
    mixed_back = jnp.stack(mixed_back).astype(F32)

    out = jax.ShapeDtypeStruct((layers, columns, shard_rows), F32)
    moment_new = pl.pallas_call(
        momentum_kernel,
        in_specs=[smem, vmem, vmem],
        out_shape=out,
        compiler_params=vmem_params(),
        cost_estimate=pl.CostEstimate(flops=10**10, bytes_accessed=2 * 10**6, transcendentals=0),
    )(jnp.stack([z, y, c]), mixed_back, momentum_t)
    ortho_back = lax.all_to_all(ortho_send, "dp", 0, 0).reshape(SIZE_Z, SIZE_Y, SIZE_C, 2 * depth, columns)
    new_weights = pl.pallas_call(
        functools.partial(weights_kernel, update_scale=0.2 * math.sqrt(max(HEAD, COLS))),
        out_shape=out,
        compiler_params=vmem_params(),
    )(ortho_back, weights_t)
    return jnp.transpose(moment_new, (0, 2, 1)), jnp.transpose(new_weights, (0, 2, 1))


def solution(mesh):
    in_specs = (
        P(None, "dp", None),
        P(None, "dp", "mp"),
        P("dp"),
        P(None, "dp", "mp"),
        P(None, "dp", "mp"),
    )
    out_specs = (P(None, "dp", "mp"), P(None, "dp", "mp"))
    small = mesh.shape["dp"] == SIZE_Z * SIZE_Y * SIZE_C and mesh.shape["mp"] == 2
    return jax.shard_map(
        block_plan if small else row_plan, mesh=mesh, in_specs=in_specs, out_specs=out_specs, check_vma=False
    )
```

```python
import functools
import math

import jax
import jax.numpy as jnp
from jax import lax
from jax.experimental import pallas as pl
from jax.experimental.pallas import tpu as pltpu
from jax.sharding import PartitionSpec as P

HEAD = 128
HEADS_WIN = 15
COLS = 1600
ITERS = 3
TILE_TOK = 64


quintic_a = 3.4445
quintic_b = -4.775
quintic_c = 2.0315
momentum_rate = 0.95
learn_rate = 0.02
weight_decay = 0.1
norm_floor = 1e-07

SIZE_Z, SIZE_Y, SIZE_C = 4, 2, 2
GAIN = 1.0 + momentum_rate
MIX = momentum_rate * momentum_rate / GAIN
BF16 = jnp.bfloat16
F32 = jnp.float32
F16 = jnp.float16
VMEM_BYTES = 20 * 1024 * 1024
CHUNK_ORDERS = ((3, 2, 1, 0), (0, 2, 3, 1), (3, 1, 0, 2), (0, 1, 2, 3))
CHUNK_STEPS = len(CHUNK_ORDERS[0])
CHUNK_SENDS = 2
NO_HEAD = -(1 << 20)
VALUE_MOST = 6.0
F16_MOST = 65504.0
HALF_HEAD = HEAD // 2


def quintic(current, reduce_gram):
    for step_index in range(ITERS):
        partial_value = jnp.einsum(
            "lshc,lsgc->lshg", current, current, preferred_element_type=jnp.float32
        )
        gram_matrix = reduce_gram(partial_value).astype(jnp.bfloat16)
        square = jnp.einsum(
            "lshg,lsgk->lshk", gram_matrix, gram_matrix, preferred_element_type=jnp.float32
        )
        poly_term = (quintic_b * gram_matrix.astype(jnp.float32) + quintic_c * square).astype(
            jnp.bfloat16
        )
        product = jnp.einsum(
            "lshg,lsgc->lshc", poly_term, current, preferred_element_type=jnp.float32
        )
        current = (quintic_a * current.astype(jnp.float32) + product).astype(jnp.bfloat16)
    return current


def row_plan(context, cotangent, tile_counts, momentum, weights):
    layers, tok_dev, all_rows = context.shape
    columns = cotangent.shape[2]
    shard_rows = momentum.shape[1]
    position = lax.broadcasted_iota(jnp.int32, (tok_dev, 1), 0)
    live_mask = (position // TILE_TOK < tile_counts[0]).astype(cotangent.dtype)
    masked = cotangent * live_mask[None]
    factor = 1.0 / math.sqrt(tok_dev * lax.axis_size("dp"))

    def layer_term(layer_index):
        block = context[layer_index]
        return (
            lax.dot_general(
                block,
                masked[layer_index],
                (((0,), (0,)), ((), ())),
                preferred_element_type=jnp.float32,
            )
            * factor
        )

    pieces = []
    for layer_index in range(layers):

        def one_term(first_row, row_count, chosen=layer_index):
            return layer_term(chosen)

        pieces.append(
            lax.psum_scatter(
                one_term(jnp.int32(0), lax.axis_size("dp") * shard_rows),
                "dp",
                scatter_dimension=0,
                tiled=True,
            )
        )
    gradient = jnp.stack(pieces)
    moment_new = momentum_rate * momentum + gradient
    nesterov = (gradient + momentum_rate * moment_new).astype(jnp.bfloat16)
    row_start = lax.axis_index("dp") * shard_rows
    slots = min(shard_rows, HEADS_WIN)
    head_ids = (row_start + lax.broadcasted_iota(jnp.int32, (slots,), 0)) % HEADS_WIN
    gathered = lax.all_gather(nesterov, "dp", axis=1, tiled=True)
    grid = gathered.reshape(layers, HEAD, HEADS_WIN, columns)
    slab_block = jnp.transpose(jnp.take(grid, head_ids, axis=2), (0, 2, 1, 3))
    widened = slab_block.astype(jnp.float32)
    sum_squares = lax.psum(jnp.sum(widened * widened, axis=(2, 3)), "mp")
    current = (widened / (jnp.sqrt(sum_squares) + norm_floor)[:, :, None, None]).astype(
        jnp.bfloat16
    )
    orthogonal = quintic(
        current,
        lambda partial_value: lax.psum(partial_value.astype(jnp.bfloat16), "mp").astype(
            jnp.float32
        ),
    )
    local_rows = lax.broadcasted_iota(jnp.int32, (shard_rows,), 0)
    global_rows = row_start + local_rows
    flat_index = local_rows % HEADS_WIN * HEAD + global_rows // HEADS_WIN
    update_rows = jnp.take(
        orthogonal.reshape(layers, slots * HEAD, columns), flat_index, axis=1
    ).astype(jnp.float32)
    update_scale = 0.2 * math.sqrt(max(HEAD, COLS))
    new_weights = weights - learn_rate * (weight_decay * weights + update_scale * update_rows)
    return (moment_new, new_weights)

def dp_index(z, y, c):
    return (z * SIZE_Y + y) * SIZE_C + c


def all_chips():
    return [(z, y, c) for z in range(SIZE_Z) for y in range(SIZE_Y) for c in range(SIZE_C)]


def swap_core(value):
    return lax.ppermute(value, "dp", [(dp_index(z, y, c), dp_index(z, y, 1 - c)) for z, y, c in all_chips()])


def swap_y(value):
    return lax.ppermute(value, "dp", [(dp_index(z, y, c), dp_index(z, 1 - y, c)) for z, y, c in all_chips()])


def swap_x(value):
    return lax.ppermute(value, "mp", [(0, 1), (1, 0)])


def after(value, *earlier):
    return lax.optimization_barrier((value, *earlier))[0]


def contract(left, right, dims):
    return lax.dot_general(left, right, (dims, ((), ())), preferred_element_type=F32)


def ext_kernel(table, counts, cotangent, momentum, send_ref, keep_ref):
    y = table[CHUNK_STEPS + 2]
    tokens, rows = cotangent.shape[2], momentum.shape[2]
    position = lax.broadcasted_iota(jnp.int32, (1, tokens), 1)
    live = (position // TILE_TOK < counts[0]).astype(F32)
    pad = jnp.zeros((send_ref.shape[0], HEAD - rows), BF16)
    for layer, out_ref in ((1 - y, send_ref), (y, keep_ref)):
        out_ref[:, :tokens] = (cotangent[layer].astype(F32) * live).astype(BF16)
        out_ref[:, tokens:] = jnp.concatenate([mixed_part(momentum[layer]), pad], axis=1)


def mixed_part(momentum):
    return (momentum * (2.0 * MIX)).astype(BF16)


def lane_lead(rows):
    row = lax.broadcasted_iota(jnp.int32, (rows, HEAD), 0)
    lane = lax.broadcasted_iota(jnp.int32, (rows, HEAD), 1)
    return row - HEADS_WIN * (lane % HALF_HEAD) - lane // HALF_HEAD


def slot_hits(lead, shift, chunk, c):
    first = chunk * 4 + c * 2
    lane = lax.broadcasted_iota(jnp.int32, lead.shape, 1)
    return (lead == first + shift) & (lane < jnp.where(first + 1 < HEADS_WIN, HEAD, HALF_HEAD))


def fill_slots(pieces, lead, table, refs, steps=range(CHUNK_STEPS)):
    lead[...] = lane_lead(lead.shape[0])
    window, columns = lead.shape[0], pieces[0].shape[-1]
    tokens = jnp.concatenate([piece[...] for piece in pieces], axis=0)
    for pair in steps[::2]:
        for half in range(2):
            first = half * (columns - window)
            shift = half * (columns // 2) - first
            places = [
                slot_hits(lead[...], shift, table[pair + index], table[CHUNK_STEPS + 3]).astype(F32).astype(BF16)
                for index in range(2)
            ]
            moved = contract(tokens[:, first : first + window], jnp.concatenate(places, axis=1), ((1,), (0,)))
            moved = moved.astype(BF16)
            for index in range(2):
                row = 0
                for ref in refs:
                    count = ref.shape[1]
                    ref[pair - steps[0] + index, :, half * HEAD : (half + 1) * HEAD] = moved[
                        row : row + count, index * HEAD : (index + 1) * HEAD
                    ]
                    row += count


def momentum_places(table, chunk, sender_y, rows, value):
    z, y, c = (table[CHUNK_STEPS + index] for index in range(1, 4))
    local = lax.broadcasted_iota(jnp.int32, (HEAD, HEAD), 0)
    lead = jnp.where(local < rows, lane_lead(HEAD), NO_HEAD)
    places = []
    for sender_c in (c, 1 - c):
        first_row = dp_index(z, sender_y, sender_c) * rows
        hits = [slot_hits(lead + first_row, half * HALF_HEAD * HEADS_WIN, chunk, c) for half in range(2)]
        hits = jnp.concatenate([jnp.where(hit, value, 0.0) for hit in hits], axis=1)
        places.append(hits.astype(BF16))
    return jnp.concatenate(places, axis=0)


def near_kernel(table, first, second, out_ref, lead):
    fill_slots((first, second), lead, table, (out_ref,))


def chip_part(ext0, ext1, tokens, places):
    count = tokens.shape[0] // 2
    total = contract(ext0[:, :count], tokens[:count], ((1,), (0,)))
    total += contract(ext1[:, :count], tokens[count:], ((1,), (0,)))
    mixed_in = jnp.concatenate([ext0[:, count:], ext1[:, count:]], axis=1)
    return total + contract(mixed_in, places, ((1,), (0,)))


def own_kernel(table, ctx0, ctx1, ext0, ext1, out_ref, lead, own, *, factor, rows):
    fill_slots((ctx0, ctx1), lead, table, (own,))
    for step in range(CHUNK_STEPS):
        places = momentum_places(table, table[step], table[CHUNK_STEPS + 2], rows, 0.5 / factor)
        out_ref[step] = chip_part(ext0[...], ext1[...], own[step], places)


def chunk_kernel(table, ext2, ext3, near, far0, far1, own, *refs, factor, rows, steps, spread):
    *out_refs, lead, far = refs
    x, y = table[CHUNK_STEPS], table[CHUNK_STEPS + 2]
    half = far0.shape[0]
    tokens = 2 * half
    fill_slots((far0, far1), lead, table, (far,), steps)
    for step, out_ref in zip(steps, out_refs):
        total = own[step]
        for source, ext in enumerate((ext2, ext3)):
            here = near[step, source * half : (source + 1) * half]
            there = far[step - steps[0], source * half : (source + 1) * half]
            low = jnp.where(x == 0, here, there)
            high = jnp.where(x == 0, there, here)
            total += contract(ext[:, :tokens], jnp.concatenate([low, high], axis=0), ((1,), (0,)))
        mixed_in = jnp.concatenate([ext2[:, tokens:], ext3[:, tokens:]], axis=1)
        total += contract(mixed_in, momentum_places(table, table[step], 1 - y, rows, 0.5 / factor), ((1,), (0,)))
        out_ref[...] = total * (factor * spread)


def head_rows(value, head):
    first, second = (value[start : start + HALF_HEAD] for start in (head * HALF_HEAD, HEAD + head * HALF_HEAD))
    return jnp.concatenate([first, second], axis=0)


def gram_kernel(mixed, near_ref, far_ref, *, spread):
    block = (GAIN / spread * mixed[...]).astype(BF16)
    total = contract(block, block, ((0,), (0,)))
    for head in range(2):
        gram = head_rows(head_rows(total, head).T, head)
        near_ref[head] = gram
        far_ref[head] = gram.astype(BF16)


def turn_kernel(mixed, turned_ref, owner_ref):
    value = mixed[...].T
    blocks = [head_rows(value, head) for head in range(2)]
    for head in range(2):
        turned_ref[head * HEAD : (head + 1) * HEAD] = blocks[head]
    store_by_owner(owner_ref, blocks)


def store_by_owner(owner_ref, blocks):
    owners = owner_ref.shape[0]
    depth = HEAD // owners
    for owner in range(owners):
        rows = [block[owner * depth : (owner + 1) * depth] for block in blocks]
        owner_ref[owner] = jnp.concatenate(rows, axis=0).astype(owner_ref.dtype)


def square_dot(left, right):
    return jnp.dot(left, right, precision=lax.Precision.HIGHEST, preferred_element_type=F32)


def ortho_kernel(near, far, turned, out_ref, *, spread):
    row = lax.broadcasted_iota(jnp.int32, (HEAD, HEAD), 0)
    column = lax.broadcasted_iota(jnp.int32, (HEAD, HEAD), 1)
    eye = (row == column).astype(F32)
    heads = range(2)
    raws = [near[head] + far[head].astype(F32) for head in heads]
    scales = [1.0 / (jnp.sqrt(jnp.sum(raw * eye, axis=(0, 1), keepdims=True)) + norm_floor) for raw in raws]
    grams = [raw * (scale * scale) for raw, scale in zip(raws, scales)]
    totals = None
    for step in range(ITERS):
        squares = [square_dot(gram, gram) for gram in grams]
        factors = [quintic_a * eye + quintic_b * gram + quintic_c * square for gram, square in zip(grams, squares)]
        totals = [square_dot(f, t) for f, t in zip(factors, totals)] if totals else factors
        if step + 1 < ITERS:
            grams = [square_dot(f, gram) for f, gram in zip(factors, grams)]
            grams = [square_dot(gram, f) for f, gram in zip(factors, grams)]
    blocks = []
    for head in heads:
        total = totals[head] * scales[head]
        high = total.astype(BF16)
        low = (total - high.astype(F32)).astype(BF16)
        block = (GAIN / spread * turned[head * HEAD : (head + 1) * HEAD]).astype(BF16)
        blocks.append(contract(high, block, ((1,), (0,))) + contract(low, block, ((1,), (0,))))
    store_by_owner(out_ref, blocks)


def to_rows(pieces):
    depth = pieces[0].shape[0] // 2
    value = jnp.concatenate(pieces, axis=0)
    row = lax.broadcasted_iota(jnp.int32, (value.shape[0], HEAD), 0)
    col = lax.broadcasted_iota(jnp.int32, (value.shape[0], HEAD), 1)
    order = (col == row % depth * HEADS_WIN + row // depth) & (row // depth < HEADS_WIN)
    order = order.astype(F32).astype(BF16)
    high = value.astype(BF16)
    result = contract(high, order, ((0,), (0,)))
    if value.dtype == F32:
        result += contract((value - high.astype(F32)).astype(BF16), order, ((0,), (0,)))
    return result


def momentum_kernel(here, mixed_back, momentum, out_ref, *, spread):
    z, y, c = (here[index] for index in range(3))
    for layer in range(2):
        old = momentum[layer]
        pieces = [
            mixed_back[(y ^ layer) * SIZE_C + (c ^ core), z ^ chip] for chip in range(SIZE_Z) for core in range(SIZE_C)
        ]
        gradient = to_rows(pieces)[:, : old.shape[1]] * (1.0 / spread) - 0.5 * mixed_part(old).astype(F32)
        out_ref[layer] = momentum_rate * old + gradient


def weights_kernel(ortho_back, weights, out_ref, *, update_scale):
    for layer in range(2):
        old = weights[layer]
        pieces = [ortho_back[chip, layer, core] for chip in range(SIZE_Z) for core in range(SIZE_C)]
        update = to_rows(pieces)[:, : old.shape[1]]
        out_ref[layer] = old - learn_rate * (weight_decay * old + update_scale * update)


def vmem_params(**kwargs):
    return pltpu.CompilerParams(vmem_limit_bytes=VMEM_BYTES, **kwargs)


def block_plan(context, cotangent, tile_counts, momentum, weights):
    layers, tok_dev, all_rows = context.shape
    columns = cotangent.shape[2]
    shard_rows = momentum.shape[1]
    depth = shard_rows // HEADS_WIN
    half = tok_dev // 2
    where = lax.axis_index("dp")
    z, y, c = where // (SIZE_Y * SIZE_C), where // SIZE_C % SIZE_Y, where % SIZE_C
    x = lax.axis_index("mp")
    factor = 1.0 / math.sqrt(tok_dev * lax.axis_size("dp"))
    spread = 2.0 ** math.floor(math.log2(F16_MOST / (VALUE_MOST**2 / factor + VALUE_MOST)))

    half_send = lax.dynamic_slice(context, (1 - y, x * half, 0), (1, half, all_rows))[0]
    first0 = swap_y(half_send)

    cotangent_t = jnp.transpose(cotangent, (0, 2, 1))
    momentum_t = jnp.transpose(momentum, (0, 2, 1))
    weights_t = jnp.transpose(weights, (0, 2, 1))
    wide = tok_dev + HEAD

    table = lax.dynamic_index_in_dim(jnp.array(CHUNK_ORDERS, jnp.int32), z, 0, False)
    table = jnp.concatenate([table, jnp.stack([x, z, y, c])])
    smem, vmem = pl.BlockSpec(memory_space=pltpu.SMEM), pl.BlockSpec(memory_space=pltpu.VMEM)
    ext_send, ext_keep = pl.pallas_call(
        ext_kernel,
        in_specs=[smem, smem, vmem, vmem],
        out_shape=[jax.ShapeDtypeStruct((columns, wide), BF16)] * 2,
        compiler_params=vmem_params(),
        cost_estimate=pl.CostEstimate(flops=10**10, bytes_accessed=2 * 10**6, transcendentals=0),
    )(after(table, half_send), tile_counts, cotangent_t, momentum_t)
    ext2 = swap_y(ext_send)
    ctx_keep = lax.dynamic_index_in_dim(context, after(y, half_send), 0, False)
    ctx1 = swap_core(ctx_keep)
    ext1 = swap_core(ext_keep)

    lanes = 2 * HEAD

    window = -(-all_rows // 2 // HEAD) * HEAD

    def planned(kernel, out_shape, *args, tokens):
        scratch = [pltpu.VMEM((window, HEAD), jnp.int32)]
        if tokens:
            scratch.append(pltpu.VMEM((CHUNK_STEPS, tokens, lanes), BF16))
        return pl.pallas_call(
            kernel,
            in_specs=[smem] + [vmem] * len(args),
            out_shape=out_shape,
            scratch_shapes=scratch,
            compiler_params=vmem_params(),
            cost_estimate=pl.CostEstimate(flops=10**3, bytes_accessed=10**3, transcendentals=0),
        )(table, *args)

    def chunks(count):
        return jax.ShapeDtypeStruct((count, columns, lanes), F32)

    first0 = after(first0, ext_keep, table)
    second0 = swap_x(first0)
    first1 = swap_core(first0)
    own = planned(
        functools.partial(own_kernel, factor=factor, rows=shard_rows),
        chunks(CHUNK_STEPS),
        after(ctx_keep, first0),
        ctx1,
        ext_keep,
        ext1,
        tokens=2 * tok_dev,
    )
    near = planned(near_kernel, jax.ShapeDtypeStruct((CHUNK_STEPS, tok_dev, lanes), BF16), first0, first1, tokens=0)
    second0 = after(second0, near, own)
    second1 = swap_core(second0)
    ext2 = after(ext2, near, own)
    ext3 = swap_core(ext2)
    one = jax.ShapeDtypeStruct((columns, lanes), F32)
    chunk = [
        planned(
            functools.partial(chunk_kernel, factor=factor, rows=shard_rows, steps=steps, spread=spread),
            [one] * len(steps),
            ext2,
            ext3,
            near,
            second0,
            second1,
            own,
            tokens=tok_dev,
        )
        for steps in (range(CHUNK_SENDS), range(CHUNK_SENDS, CHUNK_STEPS))
    ]
    chunk = [*chunk[0], *chunk[1]]

    def along_z(value, pairs):
        pairs = [(dp_index(p, b, a), dp_index(q, b, a)) for p, q in pairs for b in range(SIZE_Y) for a in range(SIZE_C)]
        return lax.ppermute(value, "dp", pairs)

    def only(condition, value):
        return jnp.where(condition, value.astype(F32), jnp.zeros((), F32))

    sent = [value.astype(F16) for value in chunk[:CHUNK_SENDS]]
    pair = along_z(sent[0], [(0, 1), (1, 0), (2, 3), (3, 2)])
    inner = along_z(sent[1], [(1, 2), (2, 1)])
    outer = along_z(sent[1], [(0, 2), (3, 1)])
    middle = (z == 1) | (z == 2)
    merged = (chunk[2] + only(middle, pair)).astype(F16)
    last = along_z(merged, [(0, 1), (1, 3), (3, 2), (2, 0)])
    base = chunk[3] + only(~middle, after(pair, merged)) + (outer.astype(F32) + inner.astype(F32))
    base, last = lax.optimization_barrier((base, last))
    mixed = base + last.astype(F32)

    owners = lax.axis_size("dp")
    by_owner = (owners, 2 * depth, columns)
    gram, gram_send = pl.pallas_call(
        functools.partial(gram_kernel, spread=spread),
        out_shape=[jax.ShapeDtypeStruct((2, HEAD, HEAD), kind) for kind in (F32, BF16)],
        compiler_params=vmem_params(),
    )(mixed)
    gram_far = swap_x(gram_send)
    turned, mixed_send = pl.pallas_call(
        turn_kernel,
        out_shape=[jax.ShapeDtypeStruct((lanes, columns), F32), jax.ShapeDtypeStruct(by_owner, F32)],
        compiler_params=vmem_params(),
        cost_estimate=pl.CostEstimate(flops=10**10, bytes_accessed=2 * 10**6, transcendentals=0),
    )(after(mixed, gram))
    ortho_send = pl.pallas_call(
        functools.partial(ortho_kernel, spread=spread),
        out_shape=jax.ShapeDtypeStruct(by_owner, BF16),
        compiler_params=vmem_params(),
    )(gram, gram_far, turned)

    mixed_send = mixed_send.astype(F16).reshape(SIZE_Z, SIZE_Y * SIZE_C, 2 * depth, columns)
    arrived = []
    for apart in range(SIZE_Z):
        piece = lax.dynamic_index_in_dim(mixed_send, z ^ apart, 0, False)
        arrived.append(along_z(piece, [(k, k ^ apart) for k in range(SIZE_Z)]) if apart else piece)
    mixed_back = []
    for apart in range(SIZE_Y * SIZE_C):
        mine = (y * SIZE_C + c) ^ apart
        piece = jnp.stack([lax.dynamic_index_in_dim(value, mine, 0, False) for value in arrived])
        if apart:
            piece = lax.ppermute(piece, "dp", [(k, k ^ apart) for k in range(owners)])
        mixed_back.append(piece)
    mixed_back = jnp.stack(mixed_back).astype(F32)

    out = jax.ShapeDtypeStruct((layers, columns, shard_rows), F32)
    moment_new = pl.pallas_call(
        functools.partial(momentum_kernel, spread=spread),
        in_specs=[smem, vmem, vmem],
        out_shape=out,
        compiler_params=vmem_params(),
        cost_estimate=pl.CostEstimate(flops=10**10, bytes_accessed=2 * 10**6, transcendentals=0),
    )(jnp.stack([z, y, c]), mixed_back, momentum_t)
    ortho_back = lax.all_to_all(ortho_send, "dp", 0, 0).reshape(SIZE_Z, SIZE_Y, SIZE_C, 2 * depth, columns)
    new_weights = pl.pallas_call(
        functools.partial(weights_kernel, update_scale=0.2 * math.sqrt(max(HEAD, COLS))),
        out_shape=out,
        compiler_params=vmem_params(),
    )(ortho_back, weights_t)
    return jnp.transpose(moment_new, (0, 2, 1)), jnp.transpose(new_weights, (0, 2, 1))


def solution(mesh):
    in_specs = (
        P(None, "dp", None),
        P(None, "dp", "mp"),
        P("dp"),
        P(None, "dp", "mp"),
        P(None, "dp", "mp"),
    )
    out_specs = (P(None, "dp", "mp"), P(None, "dp", "mp"))
    small = mesh.shape["dp"] == SIZE_Z * SIZE_Y * SIZE_C and mesh.shape["mp"] == 2
    return jax.shard_map(
        block_plan if small else row_plan, mesh=mesh, in_specs=in_specs, out_specs=out_specs, check_vma=False
    )
```

```python
import functools
import math

import jax
import jax.numpy as jnp
from jax import lax
from jax.experimental import pallas as pl
from jax.experimental.pallas import tpu as pltpu
from jax.sharding import PartitionSpec as P

HEAD = 128
HEADS_WIN = 15
COLS = 1600
ITERS = 3
TILE_TOK = 64


quintic_a = 3.4445
quintic_b = -4.775
quintic_c = 2.0315
momentum_rate = 0.95
learn_rate = 0.02
weight_decay = 0.1
norm_floor = 1e-07

SIZE_Z, SIZE_Y, SIZE_C = 4, 2, 2
GAIN = 1.0 + momentum_rate
MIX = momentum_rate * momentum_rate / GAIN
BF16 = jnp.bfloat16
F32 = jnp.float32
F16 = jnp.float16
VMEM_BYTES = 20 * 1024 * 1024
CHUNK_ORDERS = ((3, 2, 1, 0), (0, 2, 3, 1), (3, 1, 0, 2), (0, 1, 2, 3))
CHUNK_STEPS = len(CHUNK_ORDERS[0])
CHUNK_SENDS = 2
NO_HEAD = -(1 << 20)
VALUE_MOST = 6.0
F16_MOST = 65504.0
HALF_HEAD = HEAD // 2


def quintic(current, reduce_gram):
    for step_index in range(ITERS):
        partial_value = jnp.einsum(
            "lshc,lsgc->lshg", current, current, preferred_element_type=jnp.float32
        )
        gram_matrix = reduce_gram(partial_value).astype(jnp.bfloat16)
        square = jnp.einsum(
            "lshg,lsgk->lshk", gram_matrix, gram_matrix, preferred_element_type=jnp.float32
        )
        poly_term = (quintic_b * gram_matrix.astype(jnp.float32) + quintic_c * square).astype(
            jnp.bfloat16
        )
        product = jnp.einsum(
            "lshg,lsgc->lshc", poly_term, current, preferred_element_type=jnp.float32
        )
        current = (quintic_a * current.astype(jnp.float32) + product).astype(jnp.bfloat16)
    return current


def row_plan(context, cotangent, tile_counts, momentum, weights):
    layers, tok_dev, all_rows = context.shape
    columns = cotangent.shape[2]
    shard_rows = momentum.shape[1]
    position = lax.broadcasted_iota(jnp.int32, (tok_dev, 1), 0)
    live_mask = (position // TILE_TOK < tile_counts[0]).astype(cotangent.dtype)
    masked = cotangent * live_mask[None]
    factor = 1.0 / math.sqrt(tok_dev * lax.axis_size("dp"))

    def layer_term(layer_index):
        block = context[layer_index]
        return (
            lax.dot_general(
                block,
                masked[layer_index],
                (((0,), (0,)), ((), ())),
                preferred_element_type=jnp.float32,
            )
            * factor
        )

    pieces = []
    for layer_index in range(layers):

        def one_term(first_row, row_count, chosen=layer_index):
            return layer_term(chosen)

        pieces.append(
            lax.psum_scatter(
                one_term(jnp.int32(0), lax.axis_size("dp") * shard_rows),
                "dp",
                scatter_dimension=0,
                tiled=True,
            )
        )
    gradient = jnp.stack(pieces)
    moment_new = momentum_rate * momentum + gradient
    nesterov = (gradient + momentum_rate * moment_new).astype(jnp.bfloat16)
    row_start = lax.axis_index("dp") * shard_rows
    slots = min(shard_rows, HEADS_WIN)
    head_ids = (row_start + lax.broadcasted_iota(jnp.int32, (slots,), 0)) % HEADS_WIN
    gathered = lax.all_gather(nesterov, "dp", axis=1, tiled=True)
    grid = gathered.reshape(layers, HEAD, HEADS_WIN, columns)
    slab_block = jnp.transpose(jnp.take(grid, head_ids, axis=2), (0, 2, 1, 3))
    widened = slab_block.astype(jnp.float32)
    sum_squares = lax.psum(jnp.sum(widened * widened, axis=(2, 3)), "mp")
    current = (widened / (jnp.sqrt(sum_squares) + norm_floor)[:, :, None, None]).astype(
        jnp.bfloat16
    )
    orthogonal = quintic(
        current,
        lambda partial_value: lax.psum(partial_value.astype(jnp.bfloat16), "mp").astype(
            jnp.float32
        ),
    )
    local_rows = lax.broadcasted_iota(jnp.int32, (shard_rows,), 0)
    global_rows = row_start + local_rows
    flat_index = local_rows % HEADS_WIN * HEAD + global_rows // HEADS_WIN
    update_rows = jnp.take(
        orthogonal.reshape(layers, slots * HEAD, columns), flat_index, axis=1
    ).astype(jnp.float32)
    update_scale = 0.2 * math.sqrt(max(HEAD, COLS))
    new_weights = weights - learn_rate * (weight_decay * weights + update_scale * update_rows)
    return (moment_new, new_weights)

def dp_index(z, y, c):
    return (z * SIZE_Y + y) * SIZE_C + c


def all_chips():
    return [(z, y, c) for z in range(SIZE_Z) for y in range(SIZE_Y) for c in range(SIZE_C)]


def swap_core(value):
    return lax.ppermute(value, "dp", [(dp_index(z, y, c), dp_index(z, y, 1 - c)) for z, y, c in all_chips()])


def swap_y(value):
    return lax.ppermute(value, "dp", [(dp_index(z, y, c), dp_index(z, 1 - y, c)) for z, y, c in all_chips()])


def swap_x(value):
    return lax.ppermute(value, "mp", [(0, 1), (1, 0)])


def after(value, *earlier):
    return lax.optimization_barrier((value, *earlier))[0]


def contract(left, right, dims):
    return lax.dot_general(left, right, (dims, ((), ())), preferred_element_type=F32)


def ext_kernel(table, counts, cotangent, momentum, send_ref, keep_ref):
    y = table[CHUNK_STEPS + 2]
    tokens, rows = cotangent.shape[2], momentum.shape[2]
    position = lax.broadcasted_iota(jnp.int32, (1, tokens), 1)
    live = (position // TILE_TOK < counts[0]).astype(F32)
    pad = jnp.zeros((send_ref.shape[0], HEAD - rows), BF16)
    for layer, out_ref in ((1 - y, send_ref), (y, keep_ref)):
        out_ref[:, :tokens] = (cotangent[layer].astype(F32) * live).astype(BF16)
        out_ref[:, tokens:] = jnp.concatenate([mixed_part(momentum[layer]), pad], axis=1)


def mixed_part(momentum):
    return (momentum * (2.0 * MIX)).astype(BF16)


def lane_lead(rows):
    row = lax.broadcasted_iota(jnp.int32, (rows, HEAD), 0)
    lane = lax.broadcasted_iota(jnp.int32, (rows, HEAD), 1)
    return row - HEADS_WIN * (lane % HALF_HEAD) - lane // HALF_HEAD


def slot_hits(lead, shift, chunk, c):
    first = chunk * 4 + c * 2
    lane = lax.broadcasted_iota(jnp.int32, lead.shape, 1)
    return (lead == first + shift) & (lane < jnp.where(first + 1 < HEADS_WIN, HEAD, HALF_HEAD))


def fill_slots(pieces, lead, table, refs, steps=range(CHUNK_STEPS)):
    lead[...] = lane_lead(lead.shape[0])
    window, columns = lead.shape[0], pieces[0].shape[-1]
    tokens = jnp.concatenate([piece[...] for piece in pieces], axis=0)
    for pair in steps[::2]:
        for half in range(2):
            first = half * (columns - window)
            shift = half * (columns // 2) - first
            places = [
                slot_hits(lead[...], shift, table[pair + index], table[CHUNK_STEPS + 3]).astype(F32).astype(BF16)
                for index in range(2)
            ]
            moved = contract(tokens[:, first : first + window], jnp.concatenate(places, axis=1), ((1,), (0,)))
            moved = moved.astype(BF16)
            for index in range(2):
                row = 0
                for ref in refs:
                    count = ref.shape[1]
                    ref[pair - steps[0] + index, :, half * HEAD : (half + 1) * HEAD] = moved[
                        row : row + count, index * HEAD : (index + 1) * HEAD
                    ]
                    row += count


def momentum_places(table, chunk, sender_y, rows, value):
    z, y, c = (table[CHUNK_STEPS + index] for index in range(1, 4))
    local = lax.broadcasted_iota(jnp.int32, (HEAD, HEAD), 0)
    lead = jnp.where(local < rows, lane_lead(HEAD), NO_HEAD)
    places = []
    for sender_c in (c, 1 - c):
        first_row = dp_index(z, sender_y, sender_c) * rows
        hits = [slot_hits(lead + first_row, half * HALF_HEAD * HEADS_WIN, chunk, c) for half in range(2)]
        hits = jnp.concatenate([jnp.where(hit, value, 0.0) for hit in hits], axis=1)
        places.append(hits.astype(BF16))
    return jnp.concatenate(places, axis=0)


def near_kernel(table, first, second, out_ref, lead):
    fill_slots((first, second), lead, table, (out_ref,))


def chip_part(ext0, ext1, tokens, places):
    count = tokens.shape[0] // 2
    total = contract(ext0[:, :count], tokens[:count], ((1,), (0,)))
    total += contract(ext1[:, :count], tokens[count:], ((1,), (0,)))
    mixed_in = jnp.concatenate([ext0[:, count:], ext1[:, count:]], axis=1)
    return total + contract(mixed_in, places, ((1,), (0,)))


def own_kernel(table, ctx0, ctx1, ext0, ext1, out_ref, lead, own, *, factor, rows):
    fill_slots((ctx0, ctx1), lead, table, (own,))
    for step in range(CHUNK_STEPS):
        places = momentum_places(table, table[step], table[CHUNK_STEPS + 2], rows, 0.5 / factor)
        out_ref[step] = chip_part(ext0[...], ext1[...], own[step], places)


def chunk_kernel(table, ext2, ext3, near, far0, far1, own, *refs, factor, rows, steps, spread):
    *out_refs, lead, far = refs
    x, y = table[CHUNK_STEPS], table[CHUNK_STEPS + 2]
    half = far0.shape[0]
    tokens = 2 * half
    fill_slots((far0, far1), lead, table, (far,), steps)
    for step, out_ref in zip(steps, out_refs):
        total = own[step]
        for source, ext in enumerate((ext2, ext3)):
            here = near[step, source * half : (source + 1) * half]
            there = far[step - steps[0], source * half : (source + 1) * half]
            low = jnp.where(x == 0, here, there)
            high = jnp.where(x == 0, there, here)
            total += contract(ext[:, :tokens], jnp.concatenate([low, high], axis=0), ((1,), (0,)))
        mixed_in = jnp.concatenate([ext2[:, tokens:], ext3[:, tokens:]], axis=1)
        total += contract(mixed_in, momentum_places(table, table[step], 1 - y, rows, 0.5 / factor), ((1,), (0,)))
        out_ref[...] = total * (factor * spread)


def head_rows(value, head):
    first, second = (value[start : start + HALF_HEAD] for start in (head * HALF_HEAD, HEAD + head * HALF_HEAD))
    return jnp.concatenate([first, second], axis=0)


def gram_kernel(mixed, near_ref, far_ref, *, spread):
    block = (GAIN / spread * mixed[...]).astype(BF16)
    total = contract(block, block, ((0,), (0,)))
    for head in range(2):
        gram = head_rows(head_rows(total, head).T, head)
        near_ref[head] = gram
        far_ref[head] = gram.astype(BF16)


def turn_kernel(mixed, turned_ref, owner_ref):
    value = mixed[...].T
    blocks = [head_rows(value, head) for head in range(2)]
    for head in range(2):
        turned_ref[head * HEAD : (head + 1) * HEAD] = blocks[head]
    store_by_owner(owner_ref, blocks)


def store_by_owner(owner_ref, blocks):
    owners = owner_ref.shape[0]
    depth = HEAD // owners
    for owner in range(owners):
        rows = [block[owner * depth : (owner + 1) * depth] for block in blocks]
        owner_ref[owner] = jnp.concatenate(rows, axis=0).astype(owner_ref.dtype)


def square_dot(left, right):
    left_high, right_high = left.astype(BF16), right.astype(BF16)
    left_low = (left - left_high.astype(F32)).astype(BF16)
    right_low = (right - right_high.astype(F32)).astype(BF16)
    lefts = jnp.concatenate([left_high, left_low, left_high], axis=1)
    rights = jnp.concatenate([right_high, right_high, right_low], axis=0)
    return contract(lefts, rights, ((1,), (0,)))


def ortho_kernel(near, far, turned, out_ref, *, spread):
    row = lax.broadcasted_iota(jnp.int32, (HEAD, HEAD), 0)
    column = lax.broadcasted_iota(jnp.int32, (HEAD, HEAD), 1)
    eye = (row == column).astype(F32)
    heads = range(2)
    raws = [near[head] + far[head].astype(F32) for head in heads]
    scales = [1.0 / (jnp.sqrt(jnp.sum(raw * eye, axis=(0, 1), keepdims=True)) + norm_floor) for raw in raws]
    grams = [raw * (scale * scale) for raw, scale in zip(raws, scales)]
    totals = None
    for step in range(ITERS):
        squares = [square_dot(gram, gram) for gram in grams]
        factors = [quintic_a * eye + quintic_b * gram + quintic_c * square for gram, square in zip(grams, squares)]
        totals = [square_dot(f, t) for f, t in zip(factors, totals)] if totals else factors
        if step + 1 < ITERS:
            grams = [square_dot(f, gram) for f, gram in zip(factors, grams)]
            grams = [square_dot(gram, f) for f, gram in zip(factors, grams)]
    blocks = []
    for head in heads:
        total = totals[head] * scales[head]
        high = total.astype(BF16)
        low = (total - high.astype(F32)).astype(BF16)
        block = (GAIN / spread * turned[head * HEAD : (head + 1) * HEAD]).astype(BF16)
        blocks.append(contract(high, block, ((1,), (0,))) + contract(low, block, ((1,), (0,))))
    store_by_owner(out_ref, blocks)


def to_rows(pieces):
    depth = pieces[0].shape[0] // 2
    value = jnp.concatenate(pieces, axis=0)
    row = lax.broadcasted_iota(jnp.int32, (value.shape[0], HEAD), 0)
    col = lax.broadcasted_iota(jnp.int32, (value.shape[0], HEAD), 1)
    order = (col == row % depth * HEADS_WIN + row // depth) & (row // depth < HEADS_WIN)
    order = order.astype(F32).astype(BF16)
    high = value.astype(BF16)
    result = contract(high, order, ((0,), (0,)))
    if value.dtype == F32:
        result += contract((value - high.astype(F32)).astype(BF16), order, ((0,), (0,)))
    return result


def momentum_kernel(here, mixed_back, momentum, out_ref, *, spread):
    z, y, c = (here[index] for index in range(3))
    for layer in range(2):
        old = momentum[layer]
        pieces = [
            mixed_back[(y ^ layer) * SIZE_C + (c ^ core), z ^ chip] for chip in range(SIZE_Z) for core in range(SIZE_C)
        ]
        gradient = to_rows(pieces)[:, : old.shape[1]] * (1.0 / spread) - 0.5 * mixed_part(old).astype(F32)
        out_ref[layer] = momentum_rate * old + gradient


def weights_kernel(ortho_back, weights, out_ref, *, update_scale):
    for layer in range(2):
        old = weights[layer]
        pieces = [ortho_back[chip, layer, core] for chip in range(SIZE_Z) for core in range(SIZE_C)]
        update = to_rows(pieces)[:, : old.shape[1]]
        out_ref[layer] = old - learn_rate * (weight_decay * old + update_scale * update)


def vmem_params(**kwargs):
    return pltpu.CompilerParams(vmem_limit_bytes=VMEM_BYTES, **kwargs)


def block_plan(context, cotangent, tile_counts, momentum, weights):
    layers, tok_dev, all_rows = context.shape
    columns = cotangent.shape[2]
    shard_rows = momentum.shape[1]
    depth = shard_rows // HEADS_WIN
    half = tok_dev // 2
    where = lax.axis_index("dp")
    z, y, c = where // (SIZE_Y * SIZE_C), where // SIZE_C % SIZE_Y, where % SIZE_C
    x = lax.axis_index("mp")
    factor = 1.0 / math.sqrt(tok_dev * lax.axis_size("dp"))
    spread = 2.0 ** math.floor(math.log2(F16_MOST / (VALUE_MOST**2 / factor + VALUE_MOST)))

    half_send = lax.dynamic_slice(context, (1 - y, x * half, 0), (1, half, all_rows))[0]
    first0 = swap_y(half_send)

    cotangent_t = jnp.transpose(cotangent, (0, 2, 1))
    momentum_t = jnp.transpose(momentum, (0, 2, 1))
    weights_t = jnp.transpose(weights, (0, 2, 1))
    wide = tok_dev + HEAD

    table = lax.dynamic_index_in_dim(jnp.array(CHUNK_ORDERS, jnp.int32), z, 0, False)
    table = jnp.concatenate([table, jnp.stack([x, z, y, c])])
    smem, vmem = pl.BlockSpec(memory_space=pltpu.SMEM), pl.BlockSpec(memory_space=pltpu.VMEM)
    ext_send, ext_keep = pl.pallas_call(
        ext_kernel,
        in_specs=[smem, smem, vmem, vmem],
        out_shape=[jax.ShapeDtypeStruct((columns, wide), BF16)] * 2,
        compiler_params=vmem_params(),
        cost_estimate=pl.CostEstimate(flops=10**10, bytes_accessed=2 * 10**6, transcendentals=0),
    )(after(table, half_send), tile_counts, cotangent_t, momentum_t)
    ext2 = swap_y(ext_send)
    ctx_keep = lax.dynamic_index_in_dim(context, after(y, half_send), 0, False)
    ctx1 = swap_core(ctx_keep)
    ext1 = swap_core(ext_keep)

    lanes = 2 * HEAD

    window = -(-all_rows // 2 // HEAD) * HEAD

    def planned(kernel, out_shape, *args, tokens):
        scratch = [pltpu.VMEM((window, HEAD), jnp.int32)]
        if tokens:
            scratch.append(pltpu.VMEM((CHUNK_STEPS, tokens, lanes), BF16))
        return pl.pallas_call(
            kernel,
            in_specs=[smem] + [vmem] * len(args),
            out_shape=out_shape,
            scratch_shapes=scratch,
            compiler_params=vmem_params(),
            cost_estimate=pl.CostEstimate(flops=10**3, bytes_accessed=10**3, transcendentals=0),
        )(table, *args)

    def chunks(count):
        return jax.ShapeDtypeStruct((count, columns, lanes), F32)

    first0 = after(first0, ext_keep, table)
    second0 = swap_x(first0)
    first1 = swap_core(first0)
    own = planned(
        functools.partial(own_kernel, factor=factor, rows=shard_rows),
        chunks(CHUNK_STEPS),
        after(ctx_keep, first0),
        ctx1,
        ext_keep,
        ext1,
        tokens=2 * tok_dev,
    )
    near = planned(near_kernel, jax.ShapeDtypeStruct((CHUNK_STEPS, tok_dev, lanes), BF16), first0, first1, tokens=0)
    second0 = after(second0, near, own)
    second1 = swap_core(second0)
    ext2 = after(ext2, near, own)
    ext3 = swap_core(ext2)
    one = jax.ShapeDtypeStruct((columns, lanes), F32)
    chunk = [
        planned(
            functools.partial(chunk_kernel, factor=factor, rows=shard_rows, steps=steps, spread=spread),
            [one] * len(steps),
            ext2,
            ext3,
            near,
            second0,
            second1,
            own,
            tokens=tok_dev,
        )
        for steps in (range(CHUNK_SENDS), range(CHUNK_SENDS, CHUNK_STEPS))
    ]
    chunk = [*chunk[0], *chunk[1]]

    def along_z(value, pairs):
        pairs = [(dp_index(p, b, a), dp_index(q, b, a)) for p, q in pairs for b in range(SIZE_Y) for a in range(SIZE_C)]
        return lax.ppermute(value, "dp", pairs)

    def only(condition, value):
        return jnp.where(condition, value.astype(F32), jnp.zeros((), F32))

    sent = [value.astype(F16) for value in chunk[:CHUNK_SENDS]]
    pair = along_z(sent[0], [(0, 1), (1, 0), (2, 3), (3, 2)])
    inner = along_z(sent[1], [(1, 2), (2, 1)])
    outer = along_z(sent[1], [(0, 2), (3, 1)])
    middle = (z == 1) | (z == 2)
    merged = (chunk[2] + only(middle, pair)).astype(F16)
    last = along_z(merged, [(0, 1), (1, 3), (3, 2), (2, 0)])
    base = chunk[3] + only(~middle, after(pair, merged)) + (outer.astype(F32) + inner.astype(F32))
    base, last = lax.optimization_barrier((base, last))
    mixed = base + last.astype(F32)

    owners = lax.axis_size("dp")
    by_owner = (owners, 2 * depth, columns)
    gram, gram_send = pl.pallas_call(
        functools.partial(gram_kernel, spread=spread),
        out_shape=[jax.ShapeDtypeStruct((2, HEAD, HEAD), kind) for kind in (F32, BF16)],
        compiler_params=vmem_params(),
    )(mixed)
    gram_far = swap_x(gram_send)
    turned, mixed_send = pl.pallas_call(
        turn_kernel,
        out_shape=[jax.ShapeDtypeStruct((lanes, columns), F32), jax.ShapeDtypeStruct(by_owner, F32)],
        compiler_params=vmem_params(),
        cost_estimate=pl.CostEstimate(flops=10**10, bytes_accessed=2 * 10**6, transcendentals=0),
    )(after(mixed, gram))
    ortho_send = pl.pallas_call(
        functools.partial(ortho_kernel, spread=spread),
        out_shape=jax.ShapeDtypeStruct(by_owner, BF16),
        compiler_params=vmem_params(),
    )(gram, gram_far, turned)

    mixed_send = mixed_send.astype(F16).reshape(SIZE_Z, SIZE_Y * SIZE_C, 2 * depth, columns)
    arrived = []
    for apart in range(SIZE_Z):
        piece = lax.dynamic_index_in_dim(mixed_send, z ^ apart, 0, False)
        arrived.append(along_z(piece, [(k, k ^ apart) for k in range(SIZE_Z)]) if apart else piece)
    mixed_back = []
    for apart in range(SIZE_Y * SIZE_C):
        mine = (y * SIZE_C + c) ^ apart
        piece = jnp.stack([lax.dynamic_index_in_dim(value, mine, 0, False) for value in arrived])
        if apart:
            piece = lax.ppermute(piece, "dp", [(k, k ^ apart) for k in range(owners)])
        mixed_back.append(piece)
    mixed_back = jnp.stack(mixed_back).astype(F32)

    out = jax.ShapeDtypeStruct((layers, columns, shard_rows), F32)
    moment_new = pl.pallas_call(
        functools.partial(momentum_kernel, spread=spread),
        in_specs=[smem, vmem, vmem],
        out_shape=out,
        compiler_params=vmem_params(),
        cost_estimate=pl.CostEstimate(flops=10**10, bytes_accessed=2 * 10**6, transcendentals=0),
    )(jnp.stack([z, y, c]), mixed_back, momentum_t)
    ortho_back = lax.all_to_all(ortho_send, "dp", 0, 0).reshape(SIZE_Z, SIZE_Y, SIZE_C, 2 * depth, columns)
    new_weights = pl.pallas_call(
        functools.partial(weights_kernel, update_scale=0.2 * math.sqrt(max(HEAD, COLS))),
        out_shape=out,
        compiler_params=vmem_params(),
    )(ortho_back, weights_t)
    return jnp.transpose(moment_new, (0, 2, 1)), jnp.transpose(new_weights, (0, 2, 1))


def solution(mesh):
    in_specs = (
        P(None, "dp", None),
        P(None, "dp", "mp"),
        P("dp"),
        P(None, "dp", "mp"),
        P(None, "dp", "mp"),
    )
    out_specs = (P(None, "dp", "mp"), P(None, "dp", "mp"))
    small = mesh.shape["dp"] == SIZE_Z * SIZE_Y * SIZE_C and mesh.shape["mp"] == 2
    return jax.shard_map(
        block_plan if small else row_plan, mesh=mesh, in_specs=in_specs, out_specs=out_specs, check_vma=False
    )
```
